128 devices in a mesh: dp: 4 (over x), fsdp: 32 (over z, y, core).
Axes of the slice: x: 4, y: 4, z: 4, core: 2. Of those that a mesh axis runs over, the one named last changes fastest.
Arguments:
- queries: bfloat16 [131072, 512], P(('dp', 'fsdp')), parts along dimension 0
- ctx_grad: bfloat16 [131072, 512], P(('dp', 'fsdp')), parts along dimension 0, may hold values from -96 to 96
- neigh_states: bfloat16 [640, 128, 8192], P(('dp', 'fsdp')), parts along dimension 0
- key_weight: bfloat16 [32768, 512], P(('dp', 'fsdp')), parts along dimension 0
- value_weight: bfloat16 [8192, 512], P('fsdp'), may hold values from -0.0625 to 0.0625
- neighbours: int32 [2048, 2], P(('dp', 'fsdp')), parts along dimension 0, may hold values from 0 to 159, as said below
Outputs:
- context: bfloat16 [131072, 512], P(('dp', 'fsdp')), parts along dimension 0
- neigh_grad: bfloat16 [640, 128, 8192], P(('dp', 'fsdp')), parts along dimension 0
The draws below stay inside these ranges and needn't reach their ends.
There are 4 independent parts, one for each index of `dp`. The reference program is written for one: setup_inputs(seed, part) draws one part's arguments, and reference() takes and returns one part's arrays. A program takes and returns all parts, laid end to end along the dimension named above; an argument that names none is the same for every part. Nothing has to cross between parts.
Inputs may be any that keep to these rules, and one draw needn't show every extreme that they name: `neighbours`: entry b names block b of neigh_states, held by fsdp index b // 5. Among the groups of one fsdp index every named block is named exactly twice, and at most 1 distinct blocks of one owner are named; some owner is named 2 * 1 times by the groups of every fsdp index.
All inputs are finite; a program needn't handle non-finite values.
Results may differ from the reference program's by a relative error of at most 0.0075.
The reference program's roundings to bfloat16 on the way count: a program that leaves them out, or rounds other values in their place, can miss the bound.
Values may be sent and summed in bfloat16 or wider, within the bound.
No kernel may reach another device: no remote copies, remote signals or barrier semaphores. Data moves between devices by JAX's collectives and lax.ppermute only.
A program may use at most 192 MiB of HBM per device.

```python
import math
import jax
import jax.numpy as jnp
from jax import lax

D = 8192
HEAD_DIM = 128
HEADS = 4
GROUP = 64
NLEN = 128
NB_DEV = 5
C_DEV = 16
CAP = 1
GROUPS = 512
TOKENS = 32768
NBLOCKS = 160
N_FSDP = 32


def draw_queries(key, part):
    key = jax.random.fold_in(key, 3)
    key_base = jax.random.fold_in(key, 0)
    result = 2.0 * jax.random.normal(key_base, (TOKENS, HEADS * HEAD_DIM), jnp.float32)
    return result.astype(jnp.bfloat16)


def draw_neigh_states(key, part):
    key = jax.random.fold_in(key, 5)
    key_base = jax.random.fold_in(key, 0)
    result = jax.random.normal(key_base, (NBLOCKS, NLEN, D), jnp.float32)
    return result.astype(jnp.bfloat16)


def draw_key_weight(key, part):
    key = jax.random.fold_in(key, 7)
    base_rows = jax.random.normal(key, (D, HEADS * HEAD_DIM), jnp.float32) / math.sqrt(D)
    return base_rows.astype(jnp.bfloat16)


def draw_neighbours(key, part):
    key = jax.random.fold_in(key, 11)
    devices = GROUPS // C_DEV
    hot_owner = jax.random.randint(jax.random.fold_in(key, 1), (), 0, devices)
    copy_ids = jnp.tile(jnp.arange(CAP, dtype=jnp.int32), devices - 1)

    def one_device(device):
        device_key = jax.random.fold_in(key, device + 100)
        key_pick, key_base, key_order = jax.random.split(device_key, 3)
        others = (hot_owner + 1 + jnp.arange(devices - 1, dtype=jnp.int32)) % devices
        cand_owner = jnp.repeat(others, CAP)
        chosen = jax.random.permutation(key_pick, (devices - 1) * CAP)[:C_DEV - CAP]
        owner_ids = jnp.concatenate([jnp.full((CAP,), hot_owner, jnp.int32), cand_owner[chosen]])
        copy_rank = jnp.concatenate([jnp.arange(CAP, dtype=jnp.int32), copy_ids[chosen]])
        base_block = jax.random.randint(key_base, (devices,), 0, NB_DEV)
        block_ids = owner_ids * NB_DEV + (base_block[owner_ids] + copy_rank) % NB_DEV
        doubled = jnp.concatenate([block_ids, block_ids])
        order = jax.random.permutation(key_order, 2 * C_DEV)
        return doubled[order].reshape(C_DEV, 2)
    result = jax.vmap(one_device)(jnp.arange(devices, dtype=jnp.int32))
    return result.reshape(GROUPS, 2).astype(jnp.int32)


def shard_levels(rng, dims, cuts, low, high):
    def one(position, parts):
        heights = jax.random.uniform(jax.random.fold_in(jax.random.fold_in(rng, 6), position), (parts,), jnp.float32, low / len(cuts), high / len(cuts))
        return jnp.repeat(jnp.exp(heights), dims[position] // parts).reshape((-1,) + (1,) * (len(dims) - position - 1))

    loudness = one(*cuts[0])
    for cut in cuts[1:]:
        loudness = loudness * one(*cut)
    return loudness


def centred(rng, dims, deviation, reach, pieces=(), kind=jnp.bfloat16):
    values = jax.random.normal(rng, dims, jnp.float32) * deviation
    if len(pieces) > 0:
        values = shard_levels(rng, dims, pieces, -0.22, 0.18) * values
    return jnp.clip(values, min=-reach, max=reach).astype(kind)


def setup_inputs(seed: int = 0, part: int = 0) -> dict:
    splits = jax.random.split(jax.random.key(seed), 7)
    own_keys = jax.random.split(jax.random.fold_in(splits[6], part), 7)
    queries = draw_queries(jax.random.fold_in(jax.random.fold_in(splits[6], part), 71), part)
    ctx_grad = centred(own_keys[1], (TOKENS, HEADS * HEAD_DIM), 16.0, 96.0, ((0, 32),))
    neigh_states = draw_neigh_states(jax.random.fold_in(jax.random.fold_in(splits[6], part), 71), part)
    key_weight = draw_key_weight(jax.random.fold_in(jax.random.fold_in(splits[6], part), 71), part)
    value_weight = centred(splits[4], (D, HEADS * HEAD_DIM), D ** -0.5, 0.0625, ((0, 32),))
    neighbours = draw_neighbours(jax.random.fold_in(jax.random.fold_in(splits[6], part), 71), part)
    return {"queries": queries, "ctx_grad": ctx_grad, "neigh_states": neigh_states, "key_weight": key_weight, "value_weight": value_weight, "neighbours": neighbours}


def reference(queries, ctx_grad, neigh_states, key_weight, value_weight, neighbours):
    inv_scale = 1.0 / math.sqrt(HEAD_DIM)
    head_width = HEADS * HEAD_DIM
    flat_rows = neigh_states.reshape(NBLOCKS * NLEN, D)
    key_rows = jnp.dot(flat_rows, key_weight, preferred_element_type=jnp.float32).astype(jnp.bfloat16)
    value_rows = jnp.dot(flat_rows, value_weight, preferred_element_type=jnp.float32).astype(jnp.bfloat16)
    key_rows = lax.optimization_barrier(key_rows).reshape(NBLOCKS, NLEN, HEADS, HEAD_DIM)
    value_rows = lax.optimization_barrier(value_rows).reshape(NBLOCKS, NLEN, HEADS, HEAD_DIM)
    group_keys = key_rows[neighbours].reshape(GROUPS, 2 * NLEN, HEADS, HEAD_DIM).astype(jnp.float32)
    group_values = value_rows[neighbours].reshape(GROUPS, 2 * NLEN, HEADS, HEAD_DIM).astype(jnp.float32)
    query_rows = queries.reshape(GROUPS, GROUP, HEADS, HEAD_DIM).astype(jnp.float32)
    grad_rows = ctx_grad.reshape(GROUPS, GROUP, HEADS, HEAD_DIM).astype(jnp.float32)
    scores = jnp.einsum('cqhd,ckhd->chqk', query_rows, group_keys) * inv_scale
    row_top = lax.optimization_barrier(jnp.max(scores, axis=-1, keepdims=True))
    expo_rows = jnp.exp(scores - row_top)
    prob_rows = expo_rows / lax.optimization_barrier(jnp.sum(expo_rows, axis=-1, keepdims=True))
    weights = lax.optimization_barrier(prob_rows.astype(jnp.bfloat16)).astype(jnp.float32)
    context = jnp.einsum('chqk,ckhd->cqhd', weights, group_values).astype(jnp.bfloat16)
    context = context.reshape(TOKENS, head_width)
    value_grads = jnp.einsum('chqk,cqhd->ckhd', weights, grad_rows)
    prob_grads = jnp.einsum('cqhd,ckhd->chqk', grad_rows, group_values)
    score_grads = prob_rows * (prob_grads - lax.optimization_barrier(jnp.sum(prob_rows * prob_grads, axis=-1, keepdims=True))) * inv_scale
    score_grads = lax.optimization_barrier(score_grads.astype(jnp.bfloat16)).astype(jnp.float32)
    key_grads = jnp.einsum('chqk,cqhd->ckhd', score_grads, query_rows)
    request_grads = jnp.stack([key_grads, value_grads], axis=2)
    request_grads = request_grads.reshape(N_FSDP, 2 * C_DEV, NLEN * 2 * head_width)
    listed = neighbours.reshape(N_FSDP, 2 * C_DEV)
    block_ids = jnp.arange(NBLOCKS, dtype=jnp.int32)

    def add_device(running, device_item):
        device_names, entry_rows = device_item
        onehot = (device_names[:, None] == block_ids[None, :]).astype(jnp.float32)
        partial_sum = jnp.dot(onehot.T, entry_rows, precision=lax.Precision.HIGHEST)
        partial_sum = lax.optimization_barrier(partial_sum.astype(jnp.bfloat16)).astype(jnp.float32)
        return (running + partial_sum, None)
    start_sum = jnp.zeros((NBLOCKS, NLEN * 2 * head_width), jnp.float32)
    summed, _ = lax.scan(add_device, start_sum, (listed, request_grads))
    block_grads = summed.astype(jnp.bfloat16).reshape(NBLOCKS * NLEN, 2 * head_width)
    key_part = block_grads[:, :head_width]
    value_part = block_grads[:, head_width:]
    neigh_grad = jnp.dot(key_part, key_weight.T, preferred_element_type=jnp.float32)
    neigh_grad = neigh_grad + jnp.dot(value_part, value_weight.T, preferred_element_type=jnp.float32)
    neigh_grad = neigh_grad.astype(jnp.bfloat16).reshape(NBLOCKS, NLEN, D)
    return (context, neigh_grad)
```

```python
import functools
import math

import jax
import jax.numpy as jnp
from jax import lax
from jax.experimental import pallas as pl
from jax.experimental.pallas import tpu as pltpu
from jax.sharding import Mesh, PartitionSpec as P

HEAD_DIM = 128
RING = 4
BF = jnp.bfloat16
F32 = jnp.float32
VMEM_LIMIT = 60 * 1024 * 1024
NT = (((1,), (1,)), ((), ()))
TN = (((0,), (0,)), ((), ()))


def shift(x, axis, by):
    return lax.ppermute(x, axis, [(i, (i + by) % RING) for i in range(RING)])


def swap(x):
    return lax.ppermute(x, "c", [(0, 1), (1, 0)])


def ring_gather(x, axis):
    half = x.shape[0] // 2
    after = shift(x, axis, -1)
    before = shift(x, axis, 1)
    far_a = shift(after[:half], axis, -1)
    far_b = shift(before[half:], axis, 1)
    return x, after, far_a, far_b, before


def small_gather(x, axis):
    return jnp.stack([x, shift(x, axis, -1), shift(x, axis, 2), shift(x, axis, 1)])


def unit_table(neighbours, y, z, c, block_count, groups):
    own = neighbours.reshape(1, -1)
    pair = jnp.concatenate([own, swap(own)], axis=0)
    names = small_gather(pair, "y").reshape(2 * RING, -1)
    entries = names.shape[1]
    owner = names // block_count
    local = names % block_count
    owner_z = owner // (2 * RING)
    owner_y = (owner // 2) % RING
    owner_c = owner % 2
    column = ((owner_z - z) % RING) * 2 + (owner_c ^ c)
    offset_y = (owner_y - y) % RING
    entry = jnp.arange(entries, dtype=jnp.int32)
    earlier = entry[None, :] < entry[:, None]
    second = jnp.any((names[:, :, None] == names[:, None, :]) & earlier[None], axis=2)

    def other(x):
        return x.reshape(2 * RING, groups, 2)[:, :, ::-1].reshape(2 * RING, entries)

    requester = jnp.arange(2 * RING, dtype=jnp.int32)[:, None]
    req_offset, req_side = requester // 2, requester % 2
    mate_offset = other(offset_y)
    mate_slot = mate_offset * 64 + (((req_offset - mate_offset) % RING) * 2 + req_side) * 8 + other(column)
    mate_second = other(second.astype(jnp.int32))
    group_row = requester * (groups * 64) + (entry // 2)[None, :] * 64
    columns = jnp.arange(2 * RING, dtype=jnp.int32)
    hit = (column[:, None, :] == columns[None, :, None]) & (offset_y == 0)[:, None, :]
    hit_a = hit & jnp.logical_not(second)[:, None, :]
    hit_b = hit & second[:, None, :]

    def pick(mask, x):
        return jnp.sum(jnp.where(mask, x[:, None, :], 0), axis=2)

    present = jnp.any(hit, axis=2).astype(jnp.int32)
    kv_row = columns[None, :] * (block_count * 128) + pick(hit_a, local) * 128
    table = jnp.stack(
        [
            present,
            kv_row,
            pick(hit_a, group_row),
            pick(hit_b, group_row),
            pick(hit_a, mate_slot),
            pick(hit_a, mate_second),
            pick(hit_b, mate_slot),
            pick(hit_b, 1 - mate_second),
        ],
        axis=2,
    )
    return table.reshape(-1)


def ring_copies(refs, buf, sems):
    own, after, far_a, far_b, before = refs
    rows = own.shape[0]
    half = rows // 2
    places = [(own, 0, rows), (after, rows, rows), (far_a, 2 * rows, half), (far_b, 2 * rows + half, half), (before, 3 * rows, rows)]
    return [
        pltpu.make_async_copy(ref, buf.at[pl.ds(start, size)], sems.at[i])
        for i, (ref, start, size) in enumerate(places)
    ]


def load_unit(table, u, qbuf, kvbuf):
    kv_row = pl.multiple_of(table[u * 8 + 1], 128)
    row_a = pl.multiple_of(table[u * 8 + 2], 64)
    row_b = pl.multiple_of(table[u * 8 + 3], 64)
    qg = jnp.concatenate([qbuf[pl.ds(row_a, 64), :], qbuf[pl.ds(row_b, 64), :]], axis=0)
    kv = kvbuf[pl.ds(kv_row, 128), :]
    return kv_row, row_a, row_b, qg, kv


def head_parts(qg, kv, h, heads):
    width = heads * HEAD_DIM
    a, b = h * HEAD_DIM, (h + 1) * HEAD_DIM
    return qg[:, a:b], qg[:, width + a : width + b], kv[:, a:b], kv[:, width + a : width + b]


def stats_kernel(heads, table, *refs):
    q_refs, kv_refs = refs[:5], refs[5:10]
    stats, qbuf, kvbuf, qsem, ksem = refs[10:]
    copies = ring_copies(q_refs, qbuf, qsem) + ring_copies(kv_refs, kvbuf, ksem)
    for copy in copies:
        copy.start()
    for copy in copies:
        copy.wait()
    scale = 1.0 / math.sqrt(HEAD_DIM)

    def step(u, carry):
        @pl.when(table[u * 8] == 1)
        def _():
            _, _, _, qg, kv = load_unit(table, u, qbuf, kvbuf)
            rows = []
            for h in range(heads):
                q, g, k, v = head_parts(qg, kv, h, heads)
                scores = lax.dot_general(k, q, NT, preferred_element_type=F32) * scale
                prob_grads = lax.dot_general(v, g, NT, preferred_element_type=F32)
                top = jnp.max(scores, axis=0, keepdims=True)
                expo = jnp.exp(scores - top)
                rows += [top, jnp.sum(expo, axis=0, keepdims=True), jnp.sum(expo * prob_grads, axis=0, keepdims=True)]
            rows += [jnp.zeros_like(rows[0])] * (8 - len(rows))
            stats[u] = jnp.concatenate(rows, axis=0)

        return carry

    lax.fori_loop(0, 64, step, 0)


def grads_kernel(heads, table, *refs):
    q_refs, kv_refs, stat_refs = refs[:5], refs[5:10], refs[10:14]
    ctx_own, ctx_far, kvg_own, kvg_far = refs[14:18]
    qbuf, kvbuf, sbuf, ctx_acc, kvg_acc, qsem, ksem, ssem = refs[18:]
    copies = ring_copies(q_refs, qbuf, qsem) + ring_copies(kv_refs, kvbuf, ksem)
    copies += [pltpu.make_async_copy(ref, sbuf.at[pl.ds(64 * i, 64)], ssem.at[i]) for i, ref in enumerate(stat_refs)]
    for copy in copies:
        copy.start()
    ctx_acc[...] = jnp.zeros_like(ctx_acc)
    kvg_acc[...] = jnp.zeros_like(kvg_acc)
    for copy in copies:
        copy.wait()
    scale = 1.0 / math.sqrt(HEAD_DIM)
    width = heads * HEAD_DIM

    def step(u, carry):
        @pl.when(table[u * 8] == 1)
        def _():
            kv_row, row_a, row_b, qg, kv = load_unit(table, u, qbuf, kvbuf)
            mine = sbuf[u]
            mate_a, mate_b = sbuf[table[u * 8 + 4]], sbuf[table[u * 8 + 6]]
            mate_a = jnp.where(table[u * 8 + 5] == 1, pltpu.roll(mate_a, 64, 1), mate_a)
            mate_b = jnp.where(table[u * 8 + 7] == 1, pltpu.roll(mate_b, 64, 1), mate_b)
            lane = lax.broadcasted_iota(jnp.int32, mate_a.shape, 1)
            mate = jnp.where(lane < 64, mate_a, mate_b)
            for h in range(heads):
                q, g, k, v = head_parts(qg, kv, h, heads)
                scores = lax.dot_general(k, q, NT, preferred_element_type=F32) * scale
                prob_grads = lax.dot_general(v, g, NT, preferred_element_type=F32)
                top, total, drift = (mine[3 * h + i : 3 * h + i + 1] for i in range(3))
                top2, total2, drift2 = (mate[3 * h + i : 3 * h + i + 1] for i in range(3))
                peak = jnp.maximum(top, top2)
                part, part2 = jnp.exp(top - peak), jnp.exp(top2 - peak)
                inv = 1.0 / (total * part + total2 * part2)
                drift = (drift * part + drift2 * part2) * inv
                probs = jnp.exp(scores - peak) * inv
                weights = probs.astype(BF)
                score_grads = (probs * (prob_grads - drift) * scale).astype(BF)
                ctx = lax.dot_general(weights, v, TN, preferred_element_type=F32)
                dv = jnp.dot(weights, g, preferred_element_type=F32)
                dk = jnp.dot(score_grads, q, preferred_element_type=F32)
                a, b = h * HEAD_DIM, (h + 1) * HEAD_DIM
                ctx_acc[pl.ds(row_a, 64), a:b] += ctx[:64]
                ctx_acc[pl.ds(row_b, 64), a:b] += ctx[64:]
                kvg_acc[pl.ds(kv_row, 128), a:b] += dk.astype(BF).astype(F32)
                kvg_acc[pl.ds(kv_row, 128), width + a : width + b] += dv.astype(BF).astype(F32)

        return carry

    lax.fori_loop(0, 64, step, 0)
    ctx_rows, kv_rows = ctx_own.shape[0], kvg_own.shape[0]
    ctx_own[...] = ctx_acc[pl.ds(0, ctx_rows), :]
    kvg_own[...] = kvg_acc[pl.ds(0, kv_rows), :]
    for i in range(1, RING):
        ctx_far[i - 1] = ctx_acc[pl.ds(i * ctx_rows, ctx_rows), :].astype(BF)
        kvg_far[i - 1] = kvg_acc[pl.ds(i * kv_rows, kv_rows), :].astype(BF)


ANY = pl.BlockSpec(memory_space=pl.ANY)
SMEM = pl.BlockSpec(memory_space=pltpu.SMEM)
VMEM = pl.BlockSpec(memory_space=pltpu.VMEM)
DMA = pltpu.SemaphoreType.DMA


def call_stats(table, q_parts, kv_parts, heads):
    q_rows, kv_rows, width = q_parts[0].shape[0], kv_parts[0].shape[0], q_parts[0].shape[1]
    return pl.pallas_call(
        functools.partial(stats_kernel, heads),
        out_shape=jax.ShapeDtypeStruct((64, 8, 128), F32),
        in_specs=[SMEM] + [ANY] * 10,
        out_specs=VMEM,
        scratch_shapes=[
            pltpu.VMEM((RING * q_rows, width), BF),
            pltpu.VMEM((RING * kv_rows, width), BF),
            DMA((5,)),
            DMA((5,)),
        ],
        compiler_params=pltpu.CompilerParams(vmem_limit_bytes=VMEM_LIMIT),
        name="pair_stats",
    )(table, *q_parts, *kv_parts)


def call_grads(table, q_parts, kv_parts, stat_parts, heads):
    q_rows, kv_rows, width = q_parts[0].shape[0], kv_parts[0].shape[0], q_parts[0].shape[1]
    ctx_width = heads * HEAD_DIM
    return pl.pallas_call(
        functools.partial(grads_kernel, heads),
        out_shape=[
            jax.ShapeDtypeStruct((q_rows, ctx_width), F32),
            jax.ShapeDtypeStruct((RING - 1, q_rows, ctx_width), BF),
            jax.ShapeDtypeStruct((kv_rows, width), F32),
            jax.ShapeDtypeStruct((RING - 1, kv_rows, width), BF),
        ],
        in_specs=[SMEM] + [ANY] * 14,
        out_specs=[VMEM] * 4,
        scratch_shapes=[
            pltpu.VMEM((RING * q_rows, width), BF),
            pltpu.VMEM((RING * kv_rows, width), BF),
            pltpu.VMEM((RING * 64, 8, 128), F32),
            pltpu.VMEM((RING * q_rows, ctx_width), F32),
            pltpu.VMEM((RING * kv_rows, width), F32),
            DMA((5,)),
            DMA((5,)),
            DMA((4,)),
        ],
        compiler_params=pltpu.CompilerParams(vmem_limit_bytes=VMEM_LIMIT),
        name="pair_grads",
    )(table, *q_parts, *kv_parts, *stat_parts)


def ring_sum(own, far, axis):
    a = shift(far[0], axis, 1)
    b = shift(far[1], axis, 2)
    c = shift(far[2], axis, -1)
    return (own + a.astype(F32) + b.astype(F32) + c.astype(F32)).astype(BF)


def on_device(queries, ctx_grad, neigh_states, key_weight, value_weight, neighbours):
    z, y, c = lax.axis_index("z"), lax.axis_index("y"), lax.axis_index("c")
    block_count, block_len, feat_width = neigh_states.shape
    groups = neighbours.shape[0]
    half = key_weight.shape[1] // 2
    heads = half // HEAD_DIM
    rows = block_count * block_len

    def side(x, which):
        return lax.dynamic_slice_in_dim(x, which * half, half, axis=1)

    def both(a, b, which):
        return jnp.concatenate([side(a, which), side(b, which)], axis=1)

    w_mine = both(key_weight, value_weight, c)
    w_mate = swap(both(key_weight, value_weight, 1 - c))
    w_chip = jnp.concatenate([jnp.where(c == 0, w_mine, w_mate), jnp.where(c == 0, w_mate, w_mine)], axis=0)
    weight = lax.all_gather(w_chip, ("z", "y"), axis=0, tiled=True)

    states = neigh_states.reshape(rows, feat_width)
    states_mate = swap(states)
    qg_mate = swap(both(queries, ctx_grad, 1 - c))
    qg = jnp.concatenate([both(queries, ctx_grad, c), qg_mate], axis=0)
    q_parts = ring_gather(qg, "y")
    table = unit_table(neighbours, y, z, c, block_count, groups)

    kv = jnp.concatenate(
        [
            jnp.dot(states, weight, preferred_element_type=F32).astype(BF),
            jnp.dot(states_mate, weight, preferred_element_type=F32).astype(BF),
        ],
        axis=0,
    )
    kv_parts = ring_gather(kv, "z")
    weight_mate = swap(weight)

    stats = call_stats(table, q_parts, kv_parts, heads)
    stat_parts = [stats, shift(stats, "y", -1), shift(stats, "y", 2), shift(stats, "y", 1)]
    ctx_own, ctx_far, kvg_own, kvg_far = call_grads(table, q_parts, kv_parts, stat_parts, heads)

    kvg = ring_sum(kvg_own, kvg_far, "z")
    kvg_mate = swap(kvg[rows:])
    ctx = ring_sum(ctx_own, ctx_far, "y")
    ctx_mate = swap(ctx[qg.shape[0] // 2 :])
    ctx = ctx[: qg.shape[0] // 2]
    context = jnp.concatenate([jnp.where(c == 0, ctx, ctx_mate), jnp.where(c == 0, ctx_mate, ctx)], axis=1)

    neigh_grad = lax.dot_general(kvg[:rows], weight, NT, preferred_element_type=F32)
    neigh_grad = neigh_grad + lax.dot_general(kvg_mate, weight_mate, NT, preferred_element_type=F32)
    neigh_grad = neigh_grad.astype(BF).reshape(block_count, block_len, feat_width)
    return context, neigh_grad


def solution(mesh):
    parts = mesh.devices.size // (RING * RING * 2)
    fine = Mesh(mesh.devices.reshape(parts, RING, RING, 2), ("dp", "z", "y", "c"))
    every = ("dp", "z", "y", "c")
    return jax.shard_map(
        on_device,
        mesh=fine,
        in_specs=(
            P(every, None),
            P(every, None),
            P(every, None, None),
            P(every, None),
            P(("z", "y", "c"), None),
            P(every, None),
        ),
        out_specs=(P(every, None), P(every, None, None)),
        check_vma=False,
    )
```

```python
import functools
import math

import jax
import jax.numpy as jnp
from jax import lax
from jax.experimental import pallas as pl
from jax.experimental.pallas import tpu as pltpu
from jax.sharding import Mesh, PartitionSpec as P

HEAD_DIM = 128
RING = 4
UNITS = 64
BF = jnp.bfloat16
F32 = jnp.float32
VMEM_LIMIT = 60 * 1024 * 1024
NT = (((1,), (1,)), ((), ()))
TN = (((0,), (0,)), ((), ()))
ANY = pl.BlockSpec(memory_space=pl.ANY)
SMEM = pl.BlockSpec(memory_space=pltpu.SMEM)
VMEM = pl.BlockSpec(memory_space=pltpu.VMEM)
DMA = pltpu.SemaphoreType.DMA
PARAMS = pltpu.CompilerParams(vmem_limit_bytes=VMEM_LIMIT)


def shift(x, axis, by):
    return lax.ppermute(x, axis, [(i, (i + by) % RING) for i in range(RING)])


def swap(x):
    return lax.ppermute(x, "c", [(0, 1), (1, 0)])


def tie(x, after):
    return lax.optimization_barrier((x, after))[0]


def gather_small(x, axes):
    count = lax.axis_size(axes)
    return lax.all_to_all(jnp.broadcast_to(x[None], (count, *x.shape)), axes, 0, 0, tiled=True)


def relative(parts, start):
    return jnp.roll(parts, -start, axis=0)


def ring_gather(x, axis):
    half = x.shape[0] // 2
    after = shift(x, axis, -1)
    before = shift(x, axis, 1)
    far_a = shift(after[:half], axis, -1)
    far_b = shift(before[half:], axis, 1)
    return [x, after, far_a, far_b, before]


def total_of(own, others):
    for other in others:
        own = own + other.astype(F32)
    return own.astype(BF)


def unit_table(names, at_q, at_kv, c, block_count, q_first):
    groups = names.shape[1] // 2
    entries = names.shape[1]
    owner = names // block_count
    local = names % block_count
    owner_z = owner // (2 * RING)
    owner_y = (owner // 2) % RING
    owner_c = owner % 2
    owner_q, owner_kv = (owner_z, owner_y) if q_first else (owner_y, owner_z)
    column = ((owner_kv - at_kv) % RING) * 2 + (owner_c ^ c)
    offset = (owner_q - at_q) % RING
    entry = jnp.arange(entries, dtype=jnp.int32)
    earlier = entry[None, :] < entry[:, None]
    second = jnp.any((names[:, :, None] == names[:, None, :]) & earlier[None], axis=2)

    def other(x):
        return x.reshape(2 * RING, groups, 2)[:, :, ::-1].reshape(2 * RING, entries)

    requester = jnp.arange(2 * RING, dtype=jnp.int32)[:, None]
    req_offset, req_side = requester // 2, requester % 2
    mate_offset = other(offset)
    mate_unit = (((req_offset - mate_offset) % RING) * 2 + req_side) * 8 + other(column)
    mate_slot = other(owner_q) * (UNITS + 1) + mate_unit
    mate_second = other(second.astype(jnp.int32))
    group_row = requester * (groups * 64) + (entry // 2)[None, :] * 64
    columns = jnp.arange(2 * RING, dtype=jnp.int32)
    hit = (column[:, None, :] == columns[None, :, None]) & (offset == 0)[:, None, :]
    hit_a = hit & jnp.logical_not(second)[:, None, :]
    hit_b = hit & second[:, None, :]

    def pick(mask, x):
        return jnp.sum(jnp.where(mask, x[:, None, :], 0), axis=2)

    present = jnp.any(hit, axis=2)
    kv_row = columns[None, :] * (block_count * 128) + pick(hit_a, local) * 128
    unit = requester * 8 + columns[None, :]
    rows = jnp.stack(
        [
            unit,
            kv_row,
            pick(hit_a, group_row),
            pick(hit_b, group_row),
            pick(hit_a, mate_slot),
            pick(hit_a, mate_second),
            pick(hit_b, mate_slot),
            pick(hit_b, 1 - mate_second),
        ],
        axis=2,
    ).reshape(UNITS, 8)
    present = present.reshape(UNITS)
    place = jnp.arange(UNITS, dtype=jnp.int32)
    rank = jnp.sum(present[None, :] & (place[None, :] < place[:, None]), axis=1)
    count = jnp.sum(present.astype(jnp.int32))
    chosen = (rank[None, :] == place[:, None]) & present[None, :]
    packed = jnp.sum(jnp.where(chosen[:, :, None], rows[None], 0), axis=1)
    spare_q, spare_kv = 2 * RING * groups * 64, 2 * RING * block_count * 128
    spare = jnp.array([UNITS, spare_kv, spare_q, spare_q, UNITS, 0, UNITS, 0], jnp.int32)
    packed = jnp.where((place < count)[:, None], packed, spare[None, :])
    return jnp.concatenate([packed.reshape(-1), jnp.stack([count, at_q])])


def project_kernel(head, w_key, w_value, x_own, x_mate, kv, acc):
    step = pl.program_id(0)
    rows = x_own.shape[0]

    @pl.when(step == 0)
    def _():
        acc[...] = jnp.zeros_like(acc)

    weight = jnp.concatenate([w_key[...], w_value[...]], axis=1)
    acc[:rows] += jnp.dot(x_own[...], weight, preferred_element_type=F32)
    acc[rows:] += jnp.dot(x_mate[...], weight, preferred_element_type=F32)

    @pl.when(step == pl.num_programs(0) - 1)
    def _():
        kv[...] = acc[...].astype(BF)


def project(weight, head, x_own, x_mate):
    rows, feat = x_own.shape
    heads = weight.shape[1] // (2 * HEAD_DIM)
    width = 2 * HEAD_DIM
    depth = feat // 8
    x_spec = pl.BlockSpec((rows, depth), lambda k, head: (0, k))
    return pl.pallas_call(
        project_kernel,
        grid_spec=pltpu.PrefetchScalarGridSpec(
            num_scalar_prefetch=1,
            grid=(8,),
            in_specs=[
                pl.BlockSpec((depth, HEAD_DIM), lambda k, head: (k, head[0])),
                pl.BlockSpec((depth, HEAD_DIM), lambda k, head: (k, heads + head[0])),
                x_spec,
                x_spec,
            ],
            out_specs=pl.BlockSpec((2 * rows, width), lambda k, head: (0, 0)),
            scratch_shapes=[pltpu.VMEM((2 * rows, width), F32)],
        ),
        out_shape=jax.ShapeDtypeStruct((2 * rows, width), BF),
        compiler_params=PARAMS,
        name="project",
    )(head.reshape(1), weight, weight, x_own, x_mate)


def expand_kernel(*refs):
    grads, weight, out = refs[:4], refs[4], refs[5]
    cuts = [ref[:, i * HEAD_DIM : (i + 1) * HEAD_DIM] for i in range(2) for ref in grads]
    left = jnp.concatenate(cuts, axis=1)
    out[...] = lax.dot_general(left, weight[...], NT, preferred_element_type=F32).astype(BF)


def expand(grads, weight):
    rows, width = grads[0].shape
    feat = weight.shape[0]
    cols = feat // 16
    return pl.pallas_call(
        expand_kernel,
        grid=(16,),
        out_shape=jax.ShapeDtypeStruct((rows, feat), BF),
        in_specs=[pl.BlockSpec((rows, width), lambda n: (0, 0))] * 4 + [pl.BlockSpec((cols, 4 * width), lambda n: (n, 0))],
        out_specs=pl.BlockSpec((rows, cols), lambda n: (0, n)),
        compiler_params=PARAMS,
        name="expand",
    )(*grads, weight)


def piece_copies(refs, buf, sems):
    copies, start = [], 0
    for i, ref in enumerate(refs):
        size = ref.shape[0]
        copies.append(pltpu.make_async_copy(ref, buf.at[pl.ds(start, size)], sems.at[i]))
        start += size
    return copies


def load_unit(table, u, qbuf, kvbuf):
    kv_row = pl.multiple_of(table[u * 8 + 1], 128)
    row_a = pl.multiple_of(table[u * 8 + 2], 64)
    row_b = pl.multiple_of(table[u * 8 + 3], 64)
    qg = jnp.concatenate([qbuf[pl.ds(row_a, 64), :], qbuf[pl.ds(row_b, 64), :]], axis=0)
    kv = kvbuf[pl.ds(kv_row, 128), :]
    rows = (kv_row, row_a, row_b)
    return rows, qg[:, :HEAD_DIM], qg[:, HEAD_DIM:], kv[:, :HEAD_DIM], kv[:, HEAD_DIM:]


def stats_kernel(table, *refs):
    q_refs, kv_refs = refs[:5], refs[5:10]
    stats, qbuf, kvbuf, qsem, ksem = refs[10:]
    copies = piece_copies(q_refs, qbuf, qsem) + piece_copies(kv_refs, kvbuf, ksem)
    for copy in copies:
        copy.start()
    for copy in copies:
        copy.wait()
    scale = 1.0 / math.sqrt(HEAD_DIM)

    def step(i, carry):
        results = []
        for u in (2 * i, 2 * i + 1):
            _, q, g, k, v = load_unit(table, u, qbuf, kvbuf)
            scores = lax.dot_general(k, q, NT, preferred_element_type=F32) * scale
            prob_grads = lax.dot_general(v, g, NT, preferred_element_type=F32)
            top = jnp.max(scores, axis=0, keepdims=True)
            expo = jnp.exp(scores - top)
            total = jnp.sum(expo, axis=0, keepdims=True)
            drift = jnp.sum(expo * prob_grads, axis=0, keepdims=True) / total
            results.append(jnp.concatenate([top + jnp.log(total), drift], axis=0))
        for j, result in enumerate(results):
            stats[table[(2 * i + j) * 8]] = result
        return carry

    lax.fori_loop(0, (table[UNITS * 8] + 1) // 2, step, 0)


def grads_kernel(table, *refs):
    q_refs, kv_refs, stats = refs[:5], refs[5:10], refs[10]
    ctx_out, kvg_out = refs[11], refs[12:16]
    qbuf, kvbuf, sbuf, ctx_acc, kvg_acc, qsem, ksem, ssem = refs[16:]
    copies = piece_copies(q_refs, qbuf, qsem) + piece_copies(kv_refs, kvbuf, ksem)
    copies.append(pltpu.make_async_copy(stats, sbuf, ssem))
    for copy in copies:
        copy.start()
    ctx_acc[...] = jnp.zeros_like(ctx_acc)
    kvg_acc[...] = jnp.zeros_like(kvg_acc)
    for copy in copies:
        copy.wait()
    scale = 1.0 / math.sqrt(HEAD_DIM)

    def step(i, carry):
        results = []
        for u in (2 * i, 2 * i + 1):
            rows, q, g, k, v = load_unit(table, u, qbuf, kvbuf)
            scores = lax.dot_general(k, q, NT, preferred_element_type=F32) * scale
            prob_grads = lax.dot_general(v, g, NT, preferred_element_type=F32)
            mine = sbuf[table[UNITS * 8 + 1] * (UNITS + 1) + table[u * 8]]
            mate_a, mate_b = sbuf[table[u * 8 + 4]], sbuf[table[u * 8 + 6]]
            mate_a = jnp.where(table[u * 8 + 5] == 1, pltpu.roll(mate_a, 64, 1), mate_a)
            mate_b = jnp.where(table[u * 8 + 7] == 1, pltpu.roll(mate_b, 64, 1), mate_b)
            lane = lax.broadcasted_iota(jnp.int32, mate_a.shape, 1)
            mate = jnp.where(lane < 64, mate_a, mate_b)
            peak = jnp.maximum(mine[:1], mate[:1])
            part, part2 = jnp.exp(mine[:1] - peak), jnp.exp(mate[:1] - peak)
            both = part + part2
            norm = peak + jnp.log(both)
            drift = (mine[1:] * part + mate[1:] * part2) / both
            probs = jnp.exp(scores - norm)
            weights = probs.astype(BF)
            score_grads = (probs * (prob_grads - drift) * scale).astype(BF)
            ctx = lax.dot_general(weights, v, TN, preferred_element_type=F32)
            dv = jnp.dot(weights, g, preferred_element_type=F32)
            dk = jnp.dot(score_grads, q, preferred_element_type=F32)
            kvg = jnp.concatenate([dk, dv], axis=1).astype(BF).astype(F32)
            results.append((rows, ctx, kvg))
        for (kv_row, row_a, row_b), ctx, kvg in results:
            ctx_acc[pl.ds(row_a, 64), :] += ctx[:64]
            ctx_acc[pl.ds(row_b, 64), :] += ctx[64:]
            kvg_acc[pl.ds(kv_row, 128), :] += kvg
        return carry

    lax.fori_loop(0, (table[UNITS * 8] + 1) // 2, step, 0)
    ctx_rows, kv_rows = ctx_out.shape[0] // RING, kvg_out[0].shape[0]
    for i in range(RING):
        row = pl.multiple_of(lax.rem(table[UNITS * 8 + 1] + i, RING) * ctx_rows, ctx_rows)
        ctx_out[pl.ds(row, ctx_rows), :] = ctx_acc[pl.ds(i * ctx_rows, ctx_rows), :].astype(BF)
        kvg_out[i][...] = kvg_acc[pl.ds(i * kv_rows, kv_rows), :].astype(kvg_out[i].dtype)


def call_stats(table, q_parts, kv_parts):
    q_rows, kv_rows, width = q_parts[0].shape[0], kv_parts[0].shape[0], q_parts[0].shape[1]
    return pl.pallas_call(
        stats_kernel,
        out_shape=jax.ShapeDtypeStruct((UNITS + 1, 2, HEAD_DIM), F32),
        in_specs=[SMEM] + [ANY] * 10,
        out_specs=VMEM,
        scratch_shapes=[
            pltpu.VMEM((4 * q_rows + 64, width), BF),
            pltpu.VMEM((4 * kv_rows + 128, width), BF),
            DMA((8,)),
            DMA((8,)),
        ],
        compiler_params=PARAMS,
        name="pair_stats",
    )(table, *q_parts, *kv_parts)


def call_grads(table, q_parts, kv_parts, stats):
    q_rows, kv_rows, width = q_parts[0].shape[0], kv_parts[0].shape[0], q_parts[0].shape[1]

    def shapes(rows, cols):
        return [jax.ShapeDtypeStruct((rows, cols), F32 if i == 0 else BF) for i in range(RING)]

    outs = pl.pallas_call(
        grads_kernel,
        out_shape=[jax.ShapeDtypeStruct((RING * q_rows, HEAD_DIM), BF)] + shapes(kv_rows, width),
        in_specs=[SMEM] + [ANY] * 11,
        out_specs=[VMEM] * 5,
        scratch_shapes=[
            pltpu.VMEM((4 * q_rows + 64, width), BF),
            pltpu.VMEM((4 * kv_rows + 128, width), BF),
            pltpu.VMEM(stats.shape, F32),
            pltpu.VMEM((4 * q_rows + 64, HEAD_DIM), F32),
            pltpu.VMEM((4 * kv_rows + 128, width), F32),
            DMA((8,)),
            DMA((8,)),
            DMA,
        ],
        compiler_params=PARAMS,
        name="pair_grads",
    )(table, *q_parts, *kv_parts, stats)
    return outs[0], outs[1:]


def on_device(queries, ctx_grad, neigh_states, key_weight, value_weight, neighbours):
    z, y, c = (lax.axis_index(name).astype(jnp.int32) for name in ("z", "y", "c"))
    block_count, block_len, feat_width = neigh_states.shape
    rows = block_count * block_len
    tokens = queries.shape[0]
    states = neigh_states.reshape(rows, feat_width)
    half = 2 * HEAD_DIM

    weight = lax.all_gather(jnp.concatenate([key_weight, value_weight], axis=1), ("z", "y", "c"), axis=0, tiled=True)

    def head(which):
        cut = [lax.dynamic_slice_in_dim(x, which * HEAD_DIM, HEAD_DIM, axis=1) for x in (queries, ctx_grad)]
        return jnp.concatenate(cut, axis=1)

    qg_swap = swap(jnp.concatenate([head(2 - 2 * c), head(3 - 2 * c)], axis=1))
    states_mate = swap(tie(states, qg_swap))
    qg = [jnp.concatenate([head(2 * c + h), qg_swap[:, h * half : (h + 1) * half]], axis=0) for h in range(2)]

    names = gather_small(neighbours.reshape(-1), ("z", "y", "c")).reshape(RING, RING, 2, -1)
    names = jnp.where(c == 0, names, names[:, :, ::-1])
    names_a = relative(lax.dynamic_index_in_dim(names, z, 0, False), y).reshape(2 * RING, -1)
    names_b = relative(lax.dynamic_index_in_dim(names, y, 1, False), z).reshape(2 * RING, -1)
    table_a = unit_table(names_a, y, z, c, block_count, False)
    table_b = unit_table(names_b, z, y, c, block_count, True)

    q_a = ring_gather(qg[0], "y")
    q_b = ring_gather(qg[1], "z")
    ready = tie(weight, (q_a[2], q_a[3], q_b[2], q_b[3]))
    kv_a = ring_gather(project(ready, 2 * c, states, states_mate), "z")
    kv_b = ring_gather(project(ready, 2 * c + 1, states, states_mate), "y")

    def totals(table, q_parts, kv_parts, axis):
        stats = call_stats(table, q_parts, kv_parts)
        return gather_small(stats, axis).reshape(-1, 2, HEAD_DIM)

    stats_a = totals(tie(table_a, kv_b[0]), q_a, kv_a, "y")
    ctx_a, kvg_a = call_grads(tie(table_a, (kv_b[2], kv_b[3])), q_a, kv_a, stats_a)
    near_a = [shift(kvg_a[1], "z", 1), shift(kvg_a[3], "z", -1)]
    table_b = tie(table_b, kvg_a[0])
    stats_b = totals(table_b, q_b, kv_b, "z")
    ctx_b, kvg_b = call_grads(tie(table_b, near_a), q_b, kv_b, stats_b)
    kvg_b = total_of(kvg_b[0], [shift(kvg_b[1], "y", 1), shift(kvg_b[3], "y", -1), shift(kvg_b[2], "y", 2)])
    kvg_a = total_of(kvg_a[0], [*near_a, shift(tie(kvg_a[2], near_a), "z", 2)])
    kvg_a, kvg_c = kvg_a[:rows], swap(kvg_a[rows:])
    kvg_b, kvg_d = kvg_b[:rows], swap(kvg_b[rows:])
    ctx_a = lax.psum_scatter(ctx_a, "y", scatter_dimension=0, tiled=True)
    ctx_b = lax.psum_scatter(ctx_b, "z", scatter_dimension=0, tiled=True)
    ctx = jnp.concatenate([ctx_a, ctx_b], axis=1)
    mine, mate = ctx[:tokens], swap(ctx[tokens:])
    context = jnp.concatenate([jnp.where(c == 0, mine, mate), jnp.where(c == 0, mate, mine)], axis=1)
    first = [jnp.where(c == 0, a, b) for a, b in ((kvg_a, kvg_c), (kvg_b, kvg_d))]
    last = [jnp.where(c == 0, b, a) for a, b in ((kvg_a, kvg_c), (kvg_b, kvg_d))]
    neigh_grad = expand(first + last, weight)
    return context, neigh_grad.reshape(block_count, block_len, feat_width)


def solution(mesh):
    parts = mesh.devices.size // (RING * RING * 2)
    fine = Mesh(mesh.devices.reshape(parts, RING, RING, 2), ("dp", "z", "y", "c"))
    every = ("dp", "z", "y", "c")
    return jax.shard_map(
        on_device,
        mesh=fine,
        in_specs=(
            P(every, None),
            P(every, None),
            P(every, None, None),
            P(every, None),
            P(("z", "y", "c"), None),
            P(every, None),
        ),
        out_specs=(P(every, None), P(every, None, None)),
        check_vma=False,
    )
```

```python
import functools
import math

import jax
import jax.numpy as jnp
from jax import lax
from jax.experimental import pallas as pl
from jax.experimental.pallas import tpu as pltpu
from jax.sharding import Mesh, PartitionSpec as P

HEAD_DIM = 128
RING = 4
UNITS = 64
BF = jnp.bfloat16
F32 = jnp.float32
VMEM_LIMIT = 60 * 1024 * 1024
NT = (((1,), (1,)), ((), ()))
TN = (((0,), (0,)), ((), ()))
ANY = pl.BlockSpec(memory_space=pl.ANY)
SMEM = pl.BlockSpec(memory_space=pltpu.SMEM)
VMEM = pl.BlockSpec(memory_space=pltpu.VMEM)
DMA = pltpu.SemaphoreType.DMA
PARAMS = pltpu.CompilerParams(vmem_limit_bytes=VMEM_LIMIT)


def shift(x, axis, by):
    return lax.ppermute(x, axis, [(i, (i + by) % RING) for i in range(RING)])


def swap(x):
    return lax.ppermute(x, "c", [(0, 1), (1, 0)])


def tie(x, after):
    return lax.optimization_barrier((x, after))[0]


def gather_small(x, axes):
    count = lax.axis_size(axes)
    return lax.all_to_all(jnp.broadcast_to(x[None], (count, *x.shape)), axes, 0, 0, tiled=True)


def relative(parts, start):
    return jnp.roll(parts, -start, axis=0)


def ring_gather(x, axis):
    half = x.shape[0] // 2
    after, before = shift(x, axis, -1), shift(x, axis, 1)
    return [x, after, shift(after[:half], axis, -1), shift(before[half:], axis, 1), before]


def line_gather(x, axis):
    return [x, shift(x, axis, -1), shift(x, axis, 2), shift(x, axis, 1)]


def ring_send(parts, axis):
    own, after, far, before = parts
    return own, shift(after, axis, 1), shift(before, axis, -1), shift(far, axis, 2)


def total_of(parts):
    total = parts[0]
    for part in parts[1:]:
        total = total + part.astype(F32)
    return total.astype(BF)


def unit_table(names, at_q, at_kv, c, block_count, q_first):
    groups = names.shape[1] // 2
    entries = names.shape[1]
    owner = names // block_count
    local = names % block_count
    owner_z = owner // (2 * RING)
    owner_y = (owner // 2) % RING
    owner_c = owner % 2
    owner_q, owner_kv = (owner_z, owner_y) if q_first else (owner_y, owner_z)
    column = ((owner_kv - at_kv) % RING) * 2 + (owner_c ^ c)
    offset = (owner_q - at_q) % RING
    entry = jnp.arange(entries, dtype=jnp.int32)
    earlier = entry[None, :] < entry[:, None]
    second = jnp.any((names[:, :, None] == names[:, None, :]) & earlier[None], axis=2)

    def other(x):
        return x.reshape(2 * RING, groups, 2)[:, :, ::-1].reshape(2 * RING, entries)

    requester = jnp.arange(2 * RING, dtype=jnp.int32)[:, None]
    req_offset, req_side = requester // 2, requester % 2
    mate_offset = other(offset)
    mate_unit = (((req_offset - mate_offset) % RING) * 2 + req_side) * 8 + other(column)
    mate_slot = mate_offset * (UNITS + 1) + mate_unit
    mate_second = other(second.astype(jnp.int32))
    group_row = requester * (groups * 64) + (entry // 2)[None, :] * 64
    columns = jnp.arange(2 * RING, dtype=jnp.int32)
    hit = (column[:, None, :] == columns[None, :, None]) & (offset == 0)[:, None, :]
    hit_a = hit & jnp.logical_not(second)[:, None, :]
    hit_b = hit & second[:, None, :]

    def pick(mask, x):
        return jnp.sum(jnp.where(mask, x[:, None, :], 0), axis=2)

    present = jnp.any(hit, axis=2)
    kv_row = columns[None, :] * (block_count * 128) + pick(hit_a, local) * 128
    unit = requester * 8 + columns[None, :]
    rows = jnp.stack(
        [
            unit,
            kv_row,
            pick(hit_a, group_row),
            pick(hit_b, group_row),
            pick(hit_a, mate_slot),
            pick(hit_a, mate_second),
            pick(hit_b, mate_slot),
            pick(hit_b, 1 - mate_second),
        ],
        axis=2,
    ).reshape(UNITS, 8)
    present = present.reshape(UNITS)
    place = jnp.arange(UNITS, dtype=jnp.int32)
    rank = jnp.sum(present[None, :] & (place[None, :] < place[:, None]), axis=1)
    count = jnp.sum(present.astype(jnp.int32))
    chosen = (rank[None, :] == place[:, None]) & present[None, :]
    packed = jnp.sum(jnp.where(chosen[:, :, None], rows[None], 0), axis=1)
    spare_q, spare_kv = 2 * RING * groups * 64, 2 * RING * block_count * 128
    spare = jnp.array([UNITS, spare_kv, spare_q, spare_q, UNITS, 0, UNITS, 0], jnp.int32)
    packed = jnp.where((place < count)[:, None], packed, spare[None, :])
    return jnp.concatenate([packed.reshape(-1), jnp.stack([count, at_q, at_kv])])


def project_kernel(head, w_key, w_value, x_own, x_mate, kv, acc):
    step = pl.program_id(0)
    rows = x_own.shape[0]

    @pl.when(step == 0)
    def _():
        acc[...] = jnp.zeros_like(acc)

    weight = jnp.concatenate([w_key[...], w_value[...]], axis=1)
    acc[:rows] += jnp.dot(x_own[...], weight, preferred_element_type=F32)
    acc[rows:] += jnp.dot(x_mate[...], weight, preferred_element_type=F32)

    @pl.when(step == pl.num_programs(0) - 1)
    def _():
        kv[...] = acc[...].astype(BF)


def project(weight, head, x_own, x_mate):
    rows, feat = x_own.shape
    heads = weight.shape[1] // (2 * HEAD_DIM)
    width = 2 * HEAD_DIM
    depth = feat // 4
    x_spec = pl.BlockSpec((rows, depth), lambda k, head: (0, k))
    return pl.pallas_call(
        project_kernel,
        grid_spec=pltpu.PrefetchScalarGridSpec(
            num_scalar_prefetch=1,
            grid=(4,),
            in_specs=[
                pl.BlockSpec((depth, HEAD_DIM), lambda k, head: (k, head[0])),
                pl.BlockSpec((depth, HEAD_DIM), lambda k, head: (k, heads + head[0])),
                x_spec,
                x_spec,
            ],
            out_specs=pl.BlockSpec((2 * rows, width), lambda k, head: (0, 0)),
            scratch_shapes=[pltpu.VMEM((2 * rows, width), F32)],
        ),
        out_shape=jax.ShapeDtypeStruct((2 * rows, width), BF),
        compiler_params=PARAMS,
        name="project",
    )(head.reshape(1), weight, weight, x_own, x_mate)


def expand_kernel(core, *refs):
    grads, (weight, out, left) = refs[:4], refs[4:]

    @pl.when(pl.program_id(0) == 0)
    def _():
        for i in range(2):
            parts = [ref[:, i * HEAD_DIM : (i + 1) * HEAD_DIM] for ref in grads]
            own, mate = jnp.concatenate(parts[:2], axis=1), jnp.concatenate(parts[2:], axis=1)
            start, width = i * 4 * HEAD_DIM, 2 * HEAD_DIM
            left[:, start : start + width] = jnp.where(core[0] == 0, own, mate)
            left[:, start + width : start + 2 * width] = jnp.where(core[0] == 0, mate, own)

    out[...] = lax.dot_general(left[...], weight[...], NT, preferred_element_type=F32).astype(BF)


def expand(core, grads, weight):
    rows, width = grads[0].shape
    feat = weight.shape[0]
    cols = feat // 4
    return pl.pallas_call(
        expand_kernel,
        grid=(4,),
        out_shape=jax.ShapeDtypeStruct((rows, feat), BF),
        in_specs=[SMEM]
        + [pl.BlockSpec((rows, width), lambda n: (0, 0))] * 4
        + [pl.BlockSpec((cols, 4 * width), lambda n: (n, 0))],
        out_specs=pl.BlockSpec((rows, cols), lambda n: (0, n)),
        scratch_shapes=[pltpu.VMEM((rows, 4 * width), BF)],
        compiler_params=PARAMS,
        name="expand",
    )(core.reshape(1), *grads, weight)


def piece_copies(refs, buf, sems):
    copies, start = [], 0
    for i, ref in enumerate(refs):
        size = ref.shape[0]
        copies.append(pltpu.make_async_copy(ref, buf.at[pl.ds(start, size)], sems.at[i]))
        start += size
    return copies


def load_unit(table, u, qbuf, kvbuf):
    kv_row = pl.multiple_of(table[u * 8 + 1], 128)
    row_a = pl.multiple_of(table[u * 8 + 2], 64)
    row_b = pl.multiple_of(table[u * 8 + 3], 64)
    qg = jnp.concatenate([qbuf[pl.ds(row_a, 64), :], qbuf[pl.ds(row_b, 64), :]], axis=0)
    kv = kvbuf[pl.ds(kv_row, 128), :]
    rows = (kv_row, row_a, row_b)
    return rows, qg[:, :HEAD_DIM], qg[:, HEAD_DIM:], kv[:, :HEAD_DIM], kv[:, HEAD_DIM:]


def stats_kernel(table, *refs):
    q_refs, kv_refs = refs[:5], refs[5:9]
    stats, qbuf, kvbuf, qsem, ksem = refs[9:]
    copies = piece_copies(q_refs, qbuf, qsem) + piece_copies(kv_refs, kvbuf, ksem)
    for copy in copies:
        copy.start()
    for copy in copies:
        copy.wait()
    scale = 1.0 / math.sqrt(HEAD_DIM)

    def step(i, carry):
        results = []
        for u in (2 * i, 2 * i + 1):
            _, q, g, k, v = load_unit(table, u, qbuf, kvbuf)
            scores = lax.dot_general(k, q, NT, preferred_element_type=F32) * scale
            prob_grads = lax.dot_general(v, g, NT, preferred_element_type=F32)
            top = jnp.max(scores, axis=0, keepdims=True)
            expo = jnp.exp(scores - top)
            total = jnp.sum(expo, axis=0, keepdims=True)
            drift = jnp.sum(expo * prob_grads, axis=0, keepdims=True) / total
            results.append(jnp.concatenate([top + jnp.log(total), drift], axis=0))
        for j, result in enumerate(results):
            stats[table[(2 * i + j) * 8]] = result
        return carry

    lax.fori_loop(0, (table[UNITS * 8] + 1) // 2, step, 0)


def grads_kernel(ctx_ring, kvg_ring, table, *refs):
    q_refs, kv_refs, stat_refs, refs = refs[:5], refs[5:9], refs[9:13], refs[13:]
    ctx_count, kvg_count = RING if ctx_ring else 1, RING if kvg_ring else 1
    ctx_out, kvg_out, refs = refs[:ctx_count], refs[ctx_count : ctx_count + kvg_count], refs[ctx_count + kvg_count :]
    qbuf, kvbuf, sbuf, ctx_acc, kvg_acc, qsem, ksem, ssem = refs
    copies = piece_copies(q_refs, qbuf, qsem) + piece_copies(kv_refs, kvbuf, ksem) + piece_copies(stat_refs, sbuf, ssem)
    for copy in copies:
        copy.start()
    ctx_acc[...] = jnp.zeros_like(ctx_acc)
    kvg_acc[...] = jnp.zeros_like(kvg_acc)
    for copy in copies:
        copy.wait()
    scale = 1.0 / math.sqrt(HEAD_DIM)

    def step(i, carry):
        results = []
        for u in (2 * i, 2 * i + 1):
            rows, q, g, k, v = load_unit(table, u, qbuf, kvbuf)
            scores = lax.dot_general(k, q, NT, preferred_element_type=F32) * scale
            prob_grads = lax.dot_general(v, g, NT, preferred_element_type=F32)
            mine = sbuf[table[u * 8]]
            mate_a, mate_b = sbuf[table[u * 8 + 4]], sbuf[table[u * 8 + 6]]
            mate_a = jnp.where(table[u * 8 + 5] == 1, pltpu.roll(mate_a, 64, 1), mate_a)
            mate_b = jnp.where(table[u * 8 + 7] == 1, pltpu.roll(mate_b, 64, 1), mate_b)
            lane = lax.broadcasted_iota(jnp.int32, mate_a.shape, 1)
            mate = jnp.where(lane < 64, mate_a, mate_b)
            peak = jnp.maximum(mine[:1], mate[:1])
            part, part2 = jnp.exp(mine[:1] - peak), jnp.exp(mate[:1] - peak)
            both = part + part2
            norm = peak + jnp.log(both)
            drift = (mine[1:] * part + mate[1:] * part2) / both
            probs = jnp.exp(scores - norm)
            weights = probs.astype(BF)
            score_grads = (probs * (prob_grads - drift) * scale).astype(BF)
            ctx = lax.dot_general(weights, v, TN, preferred_element_type=F32)
            dv = jnp.dot(weights, g, preferred_element_type=F32)
            dk = jnp.dot(score_grads, q, preferred_element_type=F32)
            kvg = jnp.concatenate([dk, dv], axis=1).astype(BF).astype(F32)
            results.append((rows, ctx, kvg))
        for (kv_row, row_a, row_b), ctx, kvg in results:
            ctx_acc[pl.ds(row_a, 64), :] += ctx[:64]
            ctx_acc[pl.ds(row_b, 64), :] += ctx[64:]
            kvg_acc[pl.ds(kv_row, 128), :] += kvg
        return carry

    lax.fori_loop(0, (table[UNITS * 8] + 1) // 2, step, 0)
    for outs, acc, at in ((ctx_out, ctx_acc, table[UNITS * 8 + 1]), (kvg_out, kvg_acc, table[UNITS * 8 + 2])):
        rows = outs[0].shape[0] * len(outs) // RING
        for i in range(RING):
            part = acc[pl.ds(i * rows, rows), :]
            if len(outs) == RING:
                outs[i][...] = part.astype(outs[i].dtype)
            else:
                outs[0][pl.ds(pl.multiple_of(lax.rem(at + i, RING) * rows, rows), rows), :] = part.astype(BF)


def call_stats(table, q_parts, kv_parts):
    q_rows, kv_rows, width = q_parts[0].shape[0], kv_parts[0].shape[0], q_parts[0].shape[1]
    return pl.pallas_call(
        stats_kernel,
        out_shape=jax.ShapeDtypeStruct((UNITS + 1, 2, HEAD_DIM), F32),
        in_specs=[SMEM] + [ANY] * 9,
        out_specs=VMEM,
        scratch_shapes=[
            pltpu.VMEM((4 * q_rows + 64, width), BF),
            pltpu.VMEM((4 * kv_rows + 128, width), BF),
            DMA((8,)),
            DMA((8,)),
        ],
        compiler_params=PARAMS,
        name="pair_stats",
    )(table, *q_parts, *kv_parts)


def call_grads(table, q_parts, kv_parts, stat_parts, ctx_ring, kvg_ring):
    q_rows, kv_rows, width = q_parts[0].shape[0], kv_parts[0].shape[0], q_parts[0].shape[1]

    def shapes(rows, cols, ring):
        if ring:
            return [jax.ShapeDtypeStruct((rows, cols), F32 if i == 0 else BF) for i in range(RING)]
        return [jax.ShapeDtypeStruct((RING * rows, cols), BF)]

    ctx_shape, kvg_shape = shapes(q_rows, HEAD_DIM, ctx_ring), shapes(kv_rows, width, kvg_ring)
    outs = pl.pallas_call(
        functools.partial(grads_kernel, ctx_ring, kvg_ring),
        out_shape=ctx_shape + kvg_shape,
        in_specs=[SMEM] + [ANY] * 13,
        out_specs=[VMEM] * len(ctx_shape + kvg_shape),
        scratch_shapes=[
            pltpu.VMEM((4 * q_rows + 64, width), BF),
            pltpu.VMEM((4 * kv_rows + 128, width), BF),
            pltpu.VMEM((RING * (UNITS + 1), 2, HEAD_DIM), F32),
            pltpu.VMEM((4 * q_rows + 64, HEAD_DIM), F32),
            pltpu.VMEM((4 * kv_rows + 128, width), F32),
            DMA((8,)),
            DMA((8,)),
            DMA((4,)),
        ],
        compiler_params=PARAMS,
        name="pair_grads",
    )(table, *q_parts, *kv_parts, *stat_parts)
    return outs[: len(ctx_shape)], outs[len(ctx_shape) :]


def on_device(queries, ctx_grad, neigh_states, key_weight, value_weight, neighbours):
    z, y, c = (lax.axis_index(name).astype(jnp.int32) for name in ("z", "y", "c"))
    block_count, block_len, feat_width = neigh_states.shape
    rows = block_count * block_len
    tokens = queries.shape[0]
    states = neigh_states.reshape(rows, feat_width)
    half = 2 * HEAD_DIM

    weight = lax.all_gather(jnp.concatenate([key_weight, value_weight], axis=1), ("z", "y", "c"), axis=0, tiled=True)

    def head(which):
        cut = [lax.dynamic_slice_in_dim(x, which * HEAD_DIM, HEAD_DIM, axis=1) for x in (queries, ctx_grad)]
        return jnp.concatenate(cut, axis=1)

    qg_swap = swap(jnp.concatenate([head(2 - 2 * c), head(3 - 2 * c)], axis=1))
    states_mate = swap(tie(states, qg_swap))
    qg = [jnp.concatenate([head(2 * c + h), qg_swap[:, h * half : (h + 1) * half]], axis=0) for h in range(2)]

    q_a = ring_gather(qg[0], "y")
    q_b = ring_gather(qg[1], "z")
    rings = (q_a[2], q_a[3], q_b[2], q_b[3])
    names = gather_small(tie(neighbours.reshape(-1), rings), ("z", "y", "c")).reshape(RING, RING, 2, -1)
    ready = tie(weight, names)
    names = jnp.where(c == 0, names, names[:, :, ::-1])
    names_a = relative(lax.dynamic_index_in_dim(names, z, 0, False), y).reshape(2 * RING, -1)
    names_b = relative(lax.dynamic_index_in_dim(names, y, 1, False), z).reshape(2 * RING, -1)
    table_a = unit_table(names_a, y, z, c, block_count, False)
    table_b = unit_table(names_b, z, y, c, block_count, True)

    kv_a = line_gather(project(ready, 2 * c, states, states_mate), "z")
    kv_b = line_gather(project(ready, 2 * c + 1, states, states_mate), "y")

    own_a = call_stats(table_a, q_a, kv_a)
    stats_a = line_gather(own_a, "y")
    own_b = call_stats(tie(table_b, own_a), q_b, kv_b)
    stats_b = line_gather(own_b, "z")
    ctx_a, (kvg_a,) = call_grads(tie(table_a, own_b), q_a, kv_a, stats_a, True, False)
    kvg_a = lax.psum_scatter(kvg_a, "z", scatter_dimension=0, tiled=True)
    (ctx_b,), kvg_b = call_grads(tie(table_b, own_b), q_b, kv_b, stats_b, False, True)
    ctx_b = lax.psum_scatter(ctx_b, "z", scatter_dimension=0, tiled=True)
    kvg_b = total_of(ring_send(kvg_b, "y"))
    ctx_a = ring_send(tie(ctx_a, kvg_b), "y")
    kvg_a, kvg_c = kvg_a[:rows], swap(kvg_a[rows:])
    kvg_b, kvg_d = kvg_b[:rows], swap(kvg_b[rows:])
    neigh_grad = expand(c, [kvg_a, kvg_b, kvg_c, kvg_d], weight)
    ctx = jnp.concatenate([total_of(tie(ctx_a, neigh_grad)), ctx_b], axis=1)
    mine, mate = ctx[:tokens], swap(ctx[tokens:])
    context = jnp.concatenate([jnp.where(c == 0, mine, mate), jnp.where(c == 0, mate, mine)], axis=1)
    return context, neigh_grad.reshape(block_count, block_len, feat_width)


def solution(mesh):
    parts = mesh.devices.size // (RING * RING * 2)
    fine = Mesh(mesh.devices.reshape(parts, RING, RING, 2), ("dp", "z", "y", "c"))
    every = ("dp", "z", "y", "c")
    return jax.shard_map(
        on_device,
        mesh=fine,
        in_specs=(
            P(every, None),
            P(every, None),
            P(every, None, None),
            P(every, None),
            P(("z", "y", "c"), None),
            P(every, None),
        ),
        out_specs=(P(every, None), P(every, None, None)),
        check_vma=False,
    )
```

```python
import functools
import math

import jax
import jax.numpy as jnp
from jax import lax
from jax.experimental import pallas as pl
from jax.experimental.pallas import tpu as pltpu
from jax.sharding import Mesh, PartitionSpec as P

HEAD_DIM = 128
RING = 4
UNITS = 64
WAYS = 8
BF = jnp.bfloat16
F32 = jnp.float32
VMEM_LIMIT = 60 * 1024 * 1024
NT = (((1,), (1,)), ((), ()))
TN = (((0,), (0,)), ((), ()))
ANY = pl.BlockSpec(memory_space=pl.ANY)
SMEM = pl.BlockSpec(memory_space=pltpu.SMEM)
VMEM = pl.BlockSpec(memory_space=pltpu.VMEM)
DMA = pltpu.SemaphoreType.DMA
PARAMS = pltpu.CompilerParams(vmem_limit_bytes=VMEM_LIMIT)


def shift(x, axis, by):
    return lax.ppermute(x, axis, [(i, (i + by) % RING) for i in range(RING)])


def swap(x):
    return lax.ppermute(x, "c", [(0, 1), (1, 0)])


def tie(x, after):
    return lax.optimization_barrier((x, after))[0]


def gather_small(x, axes):
    count = lax.axis_size(axes)
    return lax.all_to_all(jnp.broadcast_to(x[None], (count, *x.shape)), axes, 0, 0, tiled=True)


def relative(parts, start):
    return jnp.roll(parts, -start, axis=0)


def ring_gather(x, axis):
    half = x.shape[0] // 2
    after, before = shift(x, axis, -1), shift(x, axis, 1)
    return [x, after, shift(after[:half], axis, -1), shift(before[half:], axis, 1), before]


def line_gather(x, axis):
    return [x, shift(x, axis, -1), shift(x, axis, 2), shift(x, axis, 1)]


def ring_send(parts, axis):
    own, after, far, before = parts
    return own, shift(after, axis, 1), shift(before, axis, -1), shift(far, axis, 2)


def total_of(parts):
    total = parts[0]
    for part in parts[1:]:
        total = total + part.astype(F32)
    return total.astype(BF)


def unit_table(names, at_q, at_kv, c, block_count, q_first):
    groups = names.shape[1] // 2
    entries = names.shape[1]
    owner = names // block_count
    local = names % block_count
    owner_z = owner // (2 * RING)
    owner_y = (owner // 2) % RING
    owner_c = owner % 2
    owner_q, owner_kv = (owner_z, owner_y) if q_first else (owner_y, owner_z)
    column = ((owner_kv - at_kv) % RING) * 2 + (owner_c ^ c)
    offset = (owner_q - at_q) % RING
    entry = jnp.arange(entries, dtype=jnp.int32)
    earlier = entry[None, :] < entry[:, None]
    second = jnp.any((names[:, :, None] == names[:, None, :]) & earlier[None], axis=2)

    def other(x):
        return x.reshape(2 * RING, groups, 2)[:, :, ::-1].reshape(2 * RING, entries)

    requester = jnp.arange(2 * RING, dtype=jnp.int32)[:, None]
    req_offset, req_side = requester // 2, requester % 2
    mate_offset = other(offset)
    mate_unit = (((req_offset - mate_offset) % RING) * 2 + req_side) * 8 + other(column)
    mate_slot = mate_offset * (UNITS + 1) + mate_unit
    mate_second = other(second.astype(jnp.int32))
    group_row = requester * (groups * 64) + (entry // 2)[None, :] * 64
    columns = jnp.arange(2 * RING, dtype=jnp.int32)
    hit = (column[:, None, :] == columns[None, :, None]) & (offset == 0)[:, None, :]
    hit_a = hit & jnp.logical_not(second)[:, None, :]
    hit_b = hit & second[:, None, :]

    def pick(mask, x):
        return jnp.sum(jnp.where(mask, x[:, None, :], 0), axis=2)

    present = jnp.any(hit, axis=2)
    kv_row = columns[None, :] * (block_count * 128) + pick(hit_a, local) * 128
    unit = requester * 8 + columns[None, :]
    rows = jnp.stack(
        [
            unit,
            kv_row,
            pick(hit_a, group_row),
            pick(hit_b, group_row),
            pick(hit_a, mate_slot),
            pick(hit_a, mate_second),
            pick(hit_b, mate_slot),
            pick(hit_b, 1 - mate_second),
        ],
        axis=2,
    ).reshape(UNITS, 8)
    present = present.reshape(UNITS)
    place = jnp.arange(UNITS, dtype=jnp.int32)
    rank = jnp.sum(present[None, :] & (place[None, :] < place[:, None]), axis=1)
    count = jnp.sum(present.astype(jnp.int32))
    chosen = (rank[None, :] == place[:, None]) & present[None, :]
    packed = jnp.sum(jnp.where(chosen[:, :, None], rows[None], 0), axis=1)
    spare_q, spare_kv = 2 * RING * groups * 64, 2 * RING * block_count * 128
    spare = jnp.array([UNITS, spare_kv, spare_q, spare_q, UNITS, 0, UNITS, 0], jnp.int32)
    packed = jnp.where((place < count)[:, None], packed, spare[None, :])
    return jnp.concatenate([packed.reshape(-1), jnp.stack([count, at_q, at_kv])])


def project_kernel(head, w_key, w_value, x_own, x_mate, kv, acc):
    step = pl.program_id(0)
    rows = x_own.shape[0]

    @pl.when(step == 0)
    def _():
        acc[...] = jnp.zeros_like(acc)

    weight = jnp.concatenate([w_key[...], w_value[...]], axis=1)
    acc[:rows] += jnp.dot(x_own[...], weight, preferred_element_type=F32)
    acc[rows:] += jnp.dot(x_mate[...], weight, preferred_element_type=F32)

    @pl.when(step == pl.num_programs(0) - 1)
    def _():
        kv[...] = acc[...].astype(BF)


def project(weight, head, x_own, x_mate):
    rows, feat = x_own.shape
    heads = weight.shape[1] // (2 * HEAD_DIM)
    width = 2 * HEAD_DIM
    depth = feat // 4
    x_spec = pl.BlockSpec((rows, depth), lambda k, head: (0, k))
    return pl.pallas_call(
        project_kernel,
        grid_spec=pltpu.PrefetchScalarGridSpec(
            num_scalar_prefetch=1,
            grid=(4,),
            in_specs=[
                pl.BlockSpec((depth, HEAD_DIM), lambda k, head: (k, head[0])),
                pl.BlockSpec((depth, HEAD_DIM), lambda k, head: (k, heads + head[0])),
                x_spec,
                x_spec,
            ],
            out_specs=pl.BlockSpec((2 * rows, width), lambda k, head: (0, 0)),
            scratch_shapes=[pltpu.VMEM((2 * rows, width), F32)],
        ),
        out_shape=jax.ShapeDtypeStruct((2 * rows, width), BF),
        compiler_params=PARAMS,
        name="project",
    )(head.reshape(1), weight, weight, x_own, x_mate)


def expand_kernel(core, *refs):
    grads, (weight, out, left) = refs[:4], refs[4:]

    @pl.when(pl.program_id(0) == 0)
    def _():
        for i in range(2):
            parts = [ref[:, i * HEAD_DIM : (i + 1) * HEAD_DIM] for ref in grads]
            own, mate = jnp.concatenate(parts[:2], axis=1), jnp.concatenate(parts[2:], axis=1)
            start, width = i * 4 * HEAD_DIM, 2 * HEAD_DIM
            left[:, start : start + width] = jnp.where(core[0] == 0, own, mate)
            left[:, start + width : start + 2 * width] = jnp.where(core[0] == 0, mate, own)

    out[...] = lax.dot_general(left[...], weight[...], NT, preferred_element_type=F32).astype(BF)


def expand(core, grads, weight):
    rows, width = grads[0].shape
    feat = weight.shape[0]
    cols = feat // 4
    return pl.pallas_call(
        expand_kernel,
        grid=(4,),
        out_shape=jax.ShapeDtypeStruct((rows, feat), BF),
        in_specs=[SMEM]
        + [pl.BlockSpec((rows, width), lambda n: (0, 0))] * 4
        + [pl.BlockSpec((cols, 4 * width), lambda n: (n, 0))],
        out_specs=pl.BlockSpec((rows, cols), lambda n: (0, n)),
        scratch_shapes=[pltpu.VMEM((rows, 4 * width), BF)],
        compiler_params=PARAMS,
        name="expand",
    )(core.reshape(1), *grads, weight)


def piece_copies(refs, buf, sems):
    copies, start = [], 0
    for i, ref in enumerate(refs):
        size = ref.shape[0]
        copies.append(pltpu.make_async_copy(ref, buf.at[pl.ds(start, size)], sems.at[i]))
        start += size
    return copies


def load_unit(table, u, qbuf, kvbuf):
    kv_row = pl.multiple_of(table[u * 8 + 1], 128)
    row_a = pl.multiple_of(table[u * 8 + 2], 64)
    row_b = pl.multiple_of(table[u * 8 + 3], 64)
    qg = jnp.concatenate([qbuf[pl.ds(row_a, 64), :], qbuf[pl.ds(row_b, 64), :]], axis=0)
    kv = kvbuf[pl.ds(kv_row, 128), :]
    rows = (kv_row, row_a, row_b)
    return rows, qg[:, :HEAD_DIM], qg[:, HEAD_DIM:], kv[:, :HEAD_DIM], kv[:, HEAD_DIM:]


def stats_kernel(table, *refs):
    q_refs, kv_refs = refs[:5], refs[5:9]
    stats, qbuf, kvbuf, qsem, ksem = refs[9:]
    copies = piece_copies(q_refs, qbuf, qsem) + piece_copies(kv_refs, kvbuf, ksem)
    for copy in copies:
        copy.start()
    for copy in copies:
        copy.wait()
    scale = 1.0 / math.sqrt(HEAD_DIM)

    def step(i, carry):
        results = []
        for u in [WAYS * i + w for w in range(WAYS)]:
            _, q, g, k, v = load_unit(table, u, qbuf, kvbuf)
            scores = lax.dot_general(k, q, NT, preferred_element_type=F32) * scale
            prob_grads = lax.dot_general(v, g, NT, preferred_element_type=F32)
            top = jnp.max(scores, axis=0, keepdims=True)
            expo = jnp.exp(scores - top)
            total = jnp.sum(expo, axis=0, keepdims=True)
            drift = jnp.sum(expo * prob_grads, axis=0, keepdims=True) / total
            results.append(jnp.concatenate([top + jnp.log(total), drift], axis=0))
        for j, result in enumerate(results):
            stats[table[(WAYS * i + j) * 8]] = result
        return carry

    lax.fori_loop(0, (table[UNITS * 8] + WAYS - 1) // WAYS, step, 0)


def grads_kernel(ctx_ring, kvg_ring, table, *refs):
    q_refs, kv_refs, stat_refs, refs = refs[:5], refs[5:9], refs[9:13], refs[13:]
    ctx_count, kvg_count = RING if ctx_ring else 1, RING if kvg_ring else 1
    ctx_out, kvg_out, refs = refs[:ctx_count], refs[ctx_count : ctx_count + kvg_count], refs[ctx_count + kvg_count :]
    qbuf, kvbuf, sbuf, ctx_acc, kvg_acc, qsem, ksem, ssem = refs
    copies = piece_copies(q_refs, qbuf, qsem) + piece_copies(kv_refs, kvbuf, ksem) + piece_copies(stat_refs, sbuf, ssem)
    for copy in copies:
        copy.start()
    ctx_acc[...] = jnp.zeros_like(ctx_acc)
    kvg_acc[...] = jnp.zeros_like(kvg_acc)
    for copy in copies:
        copy.wait()
    scale = 1.0 / math.sqrt(HEAD_DIM)

    def step(i, carry):
        results = []
        for u in [WAYS * i + w for w in range(WAYS)]:
            rows, q, g, k, v = load_unit(table, u, qbuf, kvbuf)
            scores = lax.dot_general(k, q, NT, preferred_element_type=F32) * scale
            prob_grads = lax.dot_general(v, g, NT, preferred_element_type=F32)
            mine = sbuf[table[u * 8]]
            mate_a, mate_b = sbuf[table[u * 8 + 4]], sbuf[table[u * 8 + 6]]
            mate_a = jnp.where(table[u * 8 + 5] == 1, pltpu.roll(mate_a, 64, 1), mate_a)
            mate_b = jnp.where(table[u * 8 + 7] == 1, pltpu.roll(mate_b, 64, 1), mate_b)
            lane = lax.broadcasted_iota(jnp.int32, mate_a.shape, 1)
            mate = jnp.where(lane < 64, mate_a, mate_b)
            peak = jnp.maximum(mine[:1], mate[:1])
            part, part2 = jnp.exp(mine[:1] - peak), jnp.exp(mate[:1] - peak)
            both = part + part2
            norm = peak + jnp.log(both)
            drift = (mine[1:] * part + mate[1:] * part2) / both
            probs = jnp.exp(scores - norm)
            weights = probs.astype(BF)
            score_grads = (probs * (prob_grads - drift) * scale).astype(BF)
            ctx = lax.dot_general(weights, v, TN, preferred_element_type=F32)
            dv = jnp.dot(weights, g, preferred_element_type=F32)
            dk = jnp.dot(score_grads, q, preferred_element_type=F32)
            kvg = jnp.concatenate([dk, dv], axis=1).astype(BF).astype(F32)
            results.append((rows, ctx, kvg))
        for (kv_row, row_a, row_b), ctx, kvg in results:
            ctx_acc[pl.ds(row_a, 64), :] += ctx[:64]
            ctx_acc[pl.ds(row_b, 64), :] += ctx[64:]
            kvg_acc[pl.ds(kv_row, 128), :] += kvg
        return carry

    lax.fori_loop(0, (table[UNITS * 8] + WAYS - 1) // WAYS, step, 0)
    for outs, acc, at in ((ctx_out, ctx_acc, table[UNITS * 8 + 1]), (kvg_out, kvg_acc, table[UNITS * 8 + 2])):
        rows = outs[0].shape[0] * len(outs) // RING
        for i in range(RING):
            part = acc[pl.ds(i * rows, rows), :]
            if len(outs) == RING:
                outs[i][...] = part.astype(outs[i].dtype)
            else:
                outs[0][pl.ds(pl.multiple_of(lax.rem(at + i, RING) * rows, rows), rows), :] = part.astype(BF)


def call_stats(table, q_parts, kv_parts):
    q_rows, kv_rows, width = q_parts[0].shape[0], kv_parts[0].shape[0], q_parts[0].shape[1]
    return pl.pallas_call(
        stats_kernel,
        out_shape=jax.ShapeDtypeStruct((UNITS + 1, 2, HEAD_DIM), F32),
        in_specs=[SMEM] + [ANY] * 9,
        out_specs=VMEM,
        scratch_shapes=[
            pltpu.VMEM((4 * q_rows + 64, width), BF),
            pltpu.VMEM((4 * kv_rows + 128, width), BF),
            DMA((8,)),
            DMA((8,)),
        ],
        compiler_params=PARAMS,
        name="pair_stats",
    )(table, *q_parts, *kv_parts)


def call_grads(table, q_parts, kv_parts, stat_parts, ctx_ring, kvg_ring):
    q_rows, kv_rows, width = q_parts[0].shape[0], kv_parts[0].shape[0], q_parts[0].shape[1]

    def shapes(rows, cols, ring):
        if ring:
            return [jax.ShapeDtypeStruct((rows, cols), F32 if i == 0 else BF) for i in range(RING)]
        return [jax.ShapeDtypeStruct((RING * rows, cols), BF)]

    ctx_shape, kvg_shape = shapes(q_rows, HEAD_DIM, ctx_ring), shapes(kv_rows, width, kvg_ring)
    outs = pl.pallas_call(
        functools.partial(grads_kernel, ctx_ring, kvg_ring),
        out_shape=ctx_shape + kvg_shape,
        in_specs=[SMEM] + [ANY] * 13,
        out_specs=[VMEM] * len(ctx_shape + kvg_shape),
        scratch_shapes=[
            pltpu.VMEM((4 * q_rows + 64, width), BF),
            pltpu.VMEM((4 * kv_rows + 128, width), BF),
            pltpu.VMEM((RING * (UNITS + 1), 2, HEAD_DIM), F32),
            pltpu.VMEM((4 * q_rows + 64, HEAD_DIM), F32),
            pltpu.VMEM((4 * kv_rows + 128, width), F32),
            DMA((8,)),
            DMA((8,)),
            DMA((4,)),
        ],
        compiler_params=PARAMS,
        name="pair_grads",
    )(table, *q_parts, *kv_parts, *stat_parts)
    return outs[: len(ctx_shape)], outs[len(ctx_shape) :]


def on_device(queries, ctx_grad, neigh_states, key_weight, value_weight, neighbours):
    z, y, c = (lax.axis_index(name).astype(jnp.int32) for name in ("z", "y", "c"))
    block_count, block_len, feat_width = neigh_states.shape
    rows = block_count * block_len
    tokens = queries.shape[0]
    states = neigh_states.reshape(rows, feat_width)
    half = 2 * HEAD_DIM

    weight = lax.all_gather(jnp.concatenate([key_weight, value_weight], axis=1), ("z", "y", "c"), axis=0, tiled=True)

    def head(which):
        cut = [lax.dynamic_slice_in_dim(x, which * HEAD_DIM, HEAD_DIM, axis=1) for x in (queries, ctx_grad)]
        return jnp.concatenate(cut, axis=1)

    qg_swap = swap(jnp.concatenate([head(2 - 2 * c), head(3 - 2 * c)], axis=1))
    states_mate = swap(tie(states, qg_swap))
    qg = [jnp.concatenate([head(2 * c + h), qg_swap[:, h * half : (h + 1) * half]], axis=0) for h in range(2)]

    q_a = ring_gather(qg[0], "y")
    q_b = ring_gather(qg[1], "z")
    rings = (q_a[2], q_a[3], q_b[2], q_b[3])
    names = gather_small(tie(neighbours.reshape(-1), rings), ("z", "y", "c")).reshape(RING, RING, 2, -1)
    ready = tie(weight, names)
    names = jnp.where(c == 0, names, names[:, :, ::-1])
    names_a = relative(lax.dynamic_index_in_dim(names, z, 0, False), y).reshape(2 * RING, -1)
    names_b = relative(lax.dynamic_index_in_dim(names, y, 1, False), z).reshape(2 * RING, -1)
    table_a = unit_table(names_a, y, z, c, block_count, False)
    table_b = unit_table(names_b, z, y, c, block_count, True)

    kv_a = line_gather(project(ready, 2 * c, states, states_mate), "z")
    kv_b = line_gather(project(ready, 2 * c + 1, states, states_mate), "y")

    own_a = call_stats(table_a, q_a, kv_a)
    stats_a = line_gather(own_a, "y")
    own_b = call_stats(tie(table_b, own_a), q_b, kv_b)
    stats_b = line_gather(own_b, "z")
    ctx_a, (kvg_a,) = call_grads(tie(table_a, own_b), q_a, kv_a, stats_a, True, False)
    kvg_a = lax.psum_scatter(kvg_a, "z", scatter_dimension=0, tiled=True)
    (ctx_b,), kvg_b = call_grads(tie(table_b, own_b), q_b, kv_b, stats_b, False, True)
    ctx_b = lax.psum_scatter(ctx_b, "z", scatter_dimension=0, tiled=True)
    kvg_b = total_of(ring_send(kvg_b, "y"))
    ctx_a = ring_send(tie(ctx_a, kvg_b), "y")
    kvg_a, kvg_c = kvg_a[:rows], swap(kvg_a[rows:])
    kvg_b, kvg_d = kvg_b[:rows], swap(kvg_b[rows:])
    neigh_grad = expand(c, [kvg_a, kvg_b, kvg_c, kvg_d], weight)
    ctx = jnp.concatenate([total_of(tie(ctx_a, neigh_grad)), ctx_b], axis=1)
    mine, mate = ctx[:tokens], swap(ctx[tokens:])
    context = jnp.concatenate([jnp.where(c == 0, mine, mate), jnp.where(c == 0, mate, mine)], axis=1)
    return context, neigh_grad.reshape(block_count, block_len, feat_width)


def solution(mesh):
    parts = mesh.devices.size // (RING * RING * 2)
    fine = Mesh(mesh.devices.reshape(parts, RING, RING, 2), ("dp", "z", "y", "c"))
    every = ("dp", "z", "y", "c")
    return jax.shard_map(
        on_device,
        mesh=fine,
        in_specs=(
            P(every, None),
            P(every, None),
            P(every, None, None),
            P(every, None),
            P(("z", "y", "c"), None),
            P(every, None),
        ),
        out_specs=(P(every, None), P(every, None, None)),
        check_vma=False,
    )
```

```python
import functools
import math

import jax
import jax.numpy as jnp
from jax import lax
from jax.experimental import pallas as pl
from jax.experimental.pallas import tpu as pltpu
from jax.sharding import Mesh, PartitionSpec as P

HEAD_DIM = 128
RING = 4
UNITS = 64
WAYS = 8
BF = jnp.bfloat16
F32 = jnp.float32
VMEM_LIMIT = 60 * 1024 * 1024
NT = (((1,), (1,)), ((), ()))
TN = (((0,), (0,)), ((), ()))
ANY = pl.BlockSpec(memory_space=pl.ANY)
SMEM = pl.BlockSpec(memory_space=pltpu.SMEM)
VMEM = pl.BlockSpec(memory_space=pltpu.VMEM)
DMA = pltpu.SemaphoreType.DMA
PARAMS = pltpu.CompilerParams(vmem_limit_bytes=VMEM_LIMIT)


def shift(x, axis, by):
    return lax.ppermute(x, axis, [(i, (i + by) % RING) for i in range(RING)])


def swap(x):
    return lax.ppermute(x, "c", [(0, 1), (1, 0)])


def tie(x, after):
    return lax.optimization_barrier((x, after))[0]


def gather_small(x, axes):
    count = lax.axis_size(axes)
    return lax.all_to_all(jnp.broadcast_to(x[None], (count, *x.shape)), axes, 0, 0, tiled=True)


def relative(parts, start):
    return jnp.roll(parts, -start, axis=0)


def ring_gather(x, axis):
    half = x.shape[0] // 2
    after, before = shift(x, axis, -1), shift(x, axis, 1)
    return [x, after, shift(after[:half], axis, -1), shift(before[half:], axis, 1), before]


def line_gather(x, axis):
    return [x, shift(x, axis, -1), shift(x, axis, 2), shift(x, axis, 1)]


def ring_send(parts, axis):
    own, after, far, before = parts
    return own, shift(after, axis, 1), shift(before, axis, -1), shift(far, axis, 2)


def total_of(parts):
    total = parts[0]
    for part in parts[1:]:
        total = total + part.astype(F32)
    return total.astype(BF)


def unit_table(names, at_q, at_kv, c, block_count, q_first):
    groups = names.shape[1] // 2
    entries = names.shape[1]
    owner = names // block_count
    local = names % block_count
    owner_z = owner // (2 * RING)
    owner_y = (owner // 2) % RING
    owner_c = owner % 2
    owner_q, owner_kv = (owner_z, owner_y) if q_first else (owner_y, owner_z)
    column = ((owner_kv - at_kv) % RING) * 2 + (owner_c ^ c)
    offset = (owner_q - at_q) % RING
    entry = jnp.arange(entries, dtype=jnp.int32)
    earlier = entry[None, :] < entry[:, None]
    second = jnp.any((names[:, :, None] == names[:, None, :]) & earlier[None], axis=2)

    def other(x):
        return x.reshape(2 * RING, groups, 2)[:, :, ::-1].reshape(2 * RING, entries)

    requester = jnp.arange(2 * RING, dtype=jnp.int32)[:, None]
    req_offset, req_side = requester // 2, requester % 2
    mate_offset = other(offset)
    mate_unit = (((req_offset - mate_offset) % RING) * 2 + req_side) * 8 + other(column)
    mate_slot = mate_offset * (UNITS + 1) + mate_unit
    mate_second = other(second.astype(jnp.int32))
    group_row = requester * (groups * 64) + (entry // 2)[None, :] * 64
    columns = jnp.arange(2 * RING, dtype=jnp.int32)
    hit = (column[:, None, :] == columns[None, :, None]) & (offset == 0)[:, None, :]
    hit_a = hit & jnp.logical_not(second)[:, None, :]
    hit_b = hit & second[:, None, :]

    def pick(mask, x):
        return jnp.sum(jnp.where(mask, x[:, None, :], 0), axis=2)

    present = jnp.any(hit, axis=2)
    kv_row = columns[None, :] * (block_count * 128) + pick(hit_a, local) * 128
    unit = requester * 8 + columns[None, :]
    rows = jnp.stack(
        [
            unit,
            kv_row,
            pick(hit_a, group_row),
            pick(hit_b, group_row),
            pick(hit_a, mate_slot),
            pick(hit_a, mate_second),
            pick(hit_b, mate_slot),
            pick(hit_b, 1 - mate_second),
        ],
        axis=2,
    ).reshape(UNITS, 8)
    present = present.reshape(UNITS)
    place = jnp.arange(UNITS, dtype=jnp.int32)
    rank = jnp.sum(present[None, :] & (place[None, :] < place[:, None]), axis=1)
    count = jnp.sum(present.astype(jnp.int32))
    chosen = (rank[None, :] == place[:, None]) & present[None, :]
    packed = jnp.sum(jnp.where(chosen[:, :, None], rows[None], 0), axis=1)
    spare_q, spare_kv = 2 * RING * groups * 64, 2 * RING * block_count * 128
    spare = jnp.array([UNITS, spare_kv, spare_q, spare_q, UNITS, 0, UNITS, 0], jnp.int32)
    packed = jnp.where((place < count)[:, None], packed, spare[None, :])
    return jnp.concatenate([packed.reshape(-1), jnp.stack([count, at_q, at_kv])])


def project_kernel(head, w_key, w_value, x_own, x_mate, kv, acc):
    step = pl.program_id(0)
    rows = x_own.shape[0]

    @pl.when(step == 0)
    def _():
        acc[...] = jnp.zeros_like(acc)

    weight = jnp.concatenate([w_key[...], w_value[...]], axis=1)
    acc[:rows] += jnp.dot(x_own[...], weight, preferred_element_type=F32)
    acc[rows:] += jnp.dot(x_mate[...], weight, preferred_element_type=F32)

    @pl.when(step == pl.num_programs(0) - 1)
    def _():
        kv[...] = acc[...].astype(BF)


def project(weight, head, x_own, x_mate):
    rows, feat = x_own.shape
    heads = weight.shape[1] // (2 * HEAD_DIM)
    width = 2 * HEAD_DIM
    depth = feat // 4
    x_spec = pl.BlockSpec((rows, depth), lambda k, head: (0, k))
    return pl.pallas_call(
        project_kernel,
        grid_spec=pltpu.PrefetchScalarGridSpec(
            num_scalar_prefetch=1,
            grid=(4,),
            in_specs=[
                pl.BlockSpec((depth, HEAD_DIM), lambda k, head: (k, head[0])),
                pl.BlockSpec((depth, HEAD_DIM), lambda k, head: (k, heads + head[0])),
                x_spec,
                x_spec,
            ],
            out_specs=pl.BlockSpec((2 * rows, width), lambda k, head: (0, 0)),
            scratch_shapes=[pltpu.VMEM((2 * rows, width), F32)],
        ),
        out_shape=jax.ShapeDtypeStruct((2 * rows, width), BF),
        compiler_params=PARAMS,
        name="project",
    )(head.reshape(1), weight, weight, x_own, x_mate)


def expand_kernel(core, *refs):
    grads, (weight, out, left) = refs[:4], refs[4:]

    @pl.when(pl.program_id(0) == 0)
    def _():
        for i in range(2):
            parts = [ref[:, i * HEAD_DIM : (i + 1) * HEAD_DIM] for ref in grads]
            own, mate = jnp.concatenate(parts[:2], axis=1), jnp.concatenate(parts[2:], axis=1)
            start, width = i * 4 * HEAD_DIM, 2 * HEAD_DIM
            left[:, start : start + width] = jnp.where(core[0] == 0, own, mate)
            left[:, start + width : start + 2 * width] = jnp.where(core[0] == 0, mate, own)

    out[...] = lax.dot_general(left[...], weight[...], NT, preferred_element_type=F32).astype(BF)


def expand(core, grads, weight):
    rows, width = grads[0].shape
    feat = weight.shape[0]
    cols = feat // 4
    return pl.pallas_call(
        expand_kernel,
        grid=(4,),
        out_shape=jax.ShapeDtypeStruct((rows, feat), BF),
        in_specs=[SMEM]
        + [pl.BlockSpec((rows, width), lambda n: (0, 0))] * 4
        + [pl.BlockSpec((cols, 4 * width), lambda n: (n, 0))],
        out_specs=pl.BlockSpec((rows, cols), lambda n: (0, n)),
        scratch_shapes=[pltpu.VMEM((rows, 4 * width), BF)],
        compiler_params=PARAMS,
        name="expand",
    )(core.reshape(1), *grads, weight)


def piece_copies(refs, buf, sems):
    copies, start = [], 0
    for i, ref in enumerate(refs):
        size = ref.shape[0]
        copies.append(pltpu.make_async_copy(ref, buf.at[pl.ds(start, size)], sems.at[i]))
        start += size
    return copies


def load_unit(table, u, qbuf, kvbuf):
    kv_row = pl.multiple_of(table[u * 8 + 1], 128)
    row_a = pl.multiple_of(table[u * 8 + 2], 64)
    row_b = pl.multiple_of(table[u * 8 + 3], 64)
    qg = jnp.concatenate([qbuf[pl.ds(row_a, 64), :], qbuf[pl.ds(row_b, 64), :]], axis=0)
    kv = kvbuf[pl.ds(kv_row, 128), :]
    rows = (kv_row, row_a, row_b)
    return rows, qg[:, :HEAD_DIM], qg[:, HEAD_DIM:], kv[:, :HEAD_DIM], kv[:, HEAD_DIM:]


def stats_kernel(table, *refs):
    q_refs, kv_refs = refs[:5], refs[5:9]
    stats, qbuf, kvbuf, qsem, ksem = refs[9:]
    copies = piece_copies(q_refs, qbuf, qsem) + piece_copies(kv_refs, kvbuf, ksem)
    for copy in copies:
        copy.start()
    for copy in copies:
        copy.wait()
    scale = 1.0 / math.sqrt(HEAD_DIM)

    def step(i, carry):
        results = []
        for u in [WAYS * i + w for w in range(WAYS)]:
            _, q, g, k, v = load_unit(table, u, qbuf, kvbuf)
            scores = lax.dot_general(k, q, NT, preferred_element_type=F32) * scale
            prob_grads = lax.dot_general(v, g, NT, preferred_element_type=F32)
            top = jnp.max(scores, axis=0, keepdims=True)
            expo = jnp.exp(scores - top)
            total = jnp.sum(expo, axis=0, keepdims=True)
            drift = jnp.sum(expo * prob_grads, axis=0, keepdims=True) / total
            results.append(jnp.concatenate([top + jnp.log(total), drift], axis=0))
        for j, result in enumerate(results):
            stats[table[(WAYS * i + j) * 8]] = result
        return carry

    lax.fori_loop(0, (table[UNITS * 8] + WAYS - 1) // WAYS, step, 0)


def grads_kernel(ctx_ring, kvg_ring, table, *refs):
    q_refs, kv_refs, stat_refs, refs = refs[:5], refs[5:9], refs[9:13], refs[13:]
    ctx_count, kvg_count = RING if ctx_ring else 1, RING if kvg_ring else 1
    ctx_out, kvg_out, refs = refs[:ctx_count], refs[ctx_count : ctx_count + kvg_count], refs[ctx_count + kvg_count :]
    qbuf, kvbuf, sbuf, ctx_acc, kvg_acc, qsem, ksem, ssem = refs
    copies = piece_copies(q_refs, qbuf, qsem) + piece_copies(kv_refs, kvbuf, ksem) + piece_copies(stat_refs, sbuf, ssem)
    for copy in copies:
        copy.start()
    ctx_acc[...] = jnp.zeros_like(ctx_acc)
    kvg_acc[...] = jnp.zeros_like(kvg_acc)
    for copy in copies:
        copy.wait()
    scale = 1.0 / math.sqrt(HEAD_DIM)

    def step(i, carry):
        results = []
        for u in [WAYS * i + w for w in range(WAYS)]:
            rows, q, g, k, v = load_unit(table, u, qbuf, kvbuf)
            scores = lax.dot_general(k, q, NT, preferred_element_type=F32) * scale
            prob_grads = lax.dot_general(v, g, NT, preferred_element_type=F32)
            mine = sbuf[table[u * 8]]
            mate_a, mate_b = sbuf[table[u * 8 + 4]], sbuf[table[u * 8 + 6]]
            mate_a = jnp.where(table[u * 8 + 5] == 1, pltpu.roll(mate_a, 64, 1), mate_a)
            mate_b = jnp.where(table[u * 8 + 7] == 1, pltpu.roll(mate_b, 64, 1), mate_b)
            lane = lax.broadcasted_iota(jnp.int32, mate_a.shape, 1)
            mate = jnp.where(lane < 64, mate_a, mate_b)
            peak = jnp.maximum(mine[:1], mate[:1])
            part, part2 = jnp.exp(mine[:1] - peak), jnp.exp(mate[:1] - peak)
            both = part + part2
            norm = peak + jnp.log(both)
            drift = (mine[1:] * part + mate[1:] * part2) / both
            probs = jnp.exp(scores - norm)
            weights = probs.astype(BF)
            score_grads = (probs * (prob_grads - drift) * scale).astype(BF)
            ctx = lax.dot_general(weights, v, TN, preferred_element_type=F32)
            dv = jnp.dot(weights, g, preferred_element_type=F32)
            dk = jnp.dot(score_grads, q, preferred_element_type=F32)
            kvg = jnp.concatenate([dk, dv], axis=1).astype(BF).astype(F32)
            results.append((rows, ctx, kvg))
        for (kv_row, row_a, row_b), ctx, kvg in results:
            ctx_acc[pl.ds(row_a, 64), :] += ctx[:64]
            ctx_acc[pl.ds(row_b, 64), :] += ctx[64:]
            kvg_acc[pl.ds(kv_row, 128), :] += kvg
        return carry

    lax.fori_loop(0, (table[UNITS * 8] + WAYS - 1) // WAYS, step, 0)
    for outs, acc, at in ((ctx_out, ctx_acc, table[UNITS * 8 + 1]), (kvg_out, kvg_acc, table[UNITS * 8 + 2])):
        rows = outs[0].shape[0] * len(outs) // RING
        for i in range(RING):
            part = acc[pl.ds(i * rows, rows), :]
            if len(outs) == RING:
                outs[i][...] = part.astype(outs[i].dtype)
            else:
                outs[0][pl.ds(pl.multiple_of(lax.rem(at + i, RING) * rows, rows), rows), :] = part.astype(BF)


def call_stats(table, q_parts, kv_parts):
    q_rows, kv_rows, width = q_parts[0].shape[0], kv_parts[0].shape[0], q_parts[0].shape[1]
    return pl.pallas_call(
        stats_kernel,
        out_shape=jax.ShapeDtypeStruct((UNITS + 1, 2, HEAD_DIM), F32),
        in_specs=[SMEM] + [ANY] * 9,
        out_specs=VMEM,
        scratch_shapes=[
            pltpu.VMEM((4 * q_rows + 64, width), BF),
            pltpu.VMEM((4 * kv_rows + 128, width), BF),
            DMA((8,)),
            DMA((8,)),
        ],
        compiler_params=PARAMS,
        name="pair_stats",
    )(table, *q_parts, *kv_parts)


def call_grads(table, q_parts, kv_parts, stat_parts, ctx_ring, kvg_ring):
    q_rows, kv_rows, width = q_parts[0].shape[0], kv_parts[0].shape[0], q_parts[0].shape[1]

    def shapes(rows, cols, ring):
        if ring:
            return [jax.ShapeDtypeStruct((rows, cols), F32 if i == 0 else BF) for i in range(RING)]
        return [jax.ShapeDtypeStruct((RING * rows, cols), BF)]

    ctx_shape, kvg_shape = shapes(q_rows, HEAD_DIM, ctx_ring), shapes(kv_rows, width, kvg_ring)
    outs = pl.pallas_call(
        functools.partial(grads_kernel, ctx_ring, kvg_ring),
        out_shape=ctx_shape + kvg_shape,
        in_specs=[SMEM] + [ANY] * 13,
        out_specs=[VMEM] * len(ctx_shape + kvg_shape),
        scratch_shapes=[
            pltpu.VMEM((4 * q_rows + 64, width), BF),
            pltpu.VMEM((4 * kv_rows + 128, width), BF),
            pltpu.VMEM((RING * (UNITS + 1), 2, HEAD_DIM), F32),
            pltpu.VMEM((4 * q_rows + 64, HEAD_DIM), F32),
            pltpu.VMEM((4 * kv_rows + 128, width), F32),
            DMA((8,)),
            DMA((8,)),
            DMA((4,)),
        ],
        compiler_params=PARAMS,
        name="pair_grads",
    )(table, *q_parts, *kv_parts, *stat_parts)
    return outs[: len(ctx_shape)], outs[len(ctx_shape) :]


def on_device(queries, ctx_grad, neigh_states, key_weight, value_weight, neighbours):
    z, y, c = (lax.axis_index(name).astype(jnp.int32) for name in ("z", "y", "c"))
    block_count, block_len, feat_width = neigh_states.shape
    rows = block_count * block_len
    tokens = queries.shape[0]
    states = neigh_states.reshape(rows, feat_width)
    half = 2 * HEAD_DIM

    weight = lax.all_gather(jnp.concatenate([key_weight, value_weight], axis=1), ("z", "y", "c"), axis=0, tiled=True)

    def head(which):
        cut = [lax.dynamic_slice_in_dim(x, which * HEAD_DIM, HEAD_DIM, axis=1) for x in (queries, ctx_grad)]
        return jnp.concatenate(cut, axis=1)

    qg_swap = swap(jnp.concatenate([head(2 - 2 * c), head(3 - 2 * c)], axis=1))
    states_mate = swap(tie(states, qg_swap))
    qg = [jnp.concatenate([head(2 * c + h), qg_swap[:, h * half : (h + 1) * half]], axis=0) for h in range(2)]

    q_a = ring_gather(qg[0], "y")
    q_b = ring_gather(qg[1], "z")
    names = gather_small(tie(neighbours.reshape(-1), (q_a[1], q_a[4], q_b[1], q_b[4])), ("z", "y", "c")).reshape(RING, RING, 2, -1)
    names = jnp.where(c == 0, names, names[:, :, ::-1])
    names_a = relative(lax.dynamic_index_in_dim(names, z, 0, False), y).reshape(2 * RING, -1)
    names_b = relative(lax.dynamic_index_in_dim(names, y, 1, False), z).reshape(2 * RING, -1)
    table_a = unit_table(names_a, y, z, c, block_count, False)
    table_b = unit_table(names_b, z, y, c, block_count, True)

    ready = tie(weight, (table_a, table_b, q_a, q_b))
    kv_a = line_gather(project(ready, 2 * c, states, states_mate), "z")
    kv_b = line_gather(project(ready, 2 * c + 1, states, states_mate), "y")

    own_a = call_stats(table_a, q_a, kv_a)
    stats_a = line_gather(own_a, "y")
    own_b = call_stats(tie(table_b, own_a), q_b, kv_b)
    stats_b = line_gather(own_b, "z")
    ctx_a, (kvg_a,) = call_grads(tie(table_a, own_b), q_a, kv_a, stats_a, True, False)
    kvg_a = lax.psum_scatter(kvg_a, "z", scatter_dimension=0, tiled=True)
    (ctx_b,), kvg_b = call_grads(tie(table_b, own_b), q_b, kv_b, stats_b, False, True)
    ctx_b = lax.psum_scatter(ctx_b, "z", scatter_dimension=0, tiled=True)
    kvg_b = total_of(ring_send(kvg_b, "y"))
    ctx_a = ring_send(tie(ctx_a, kvg_b), "y")
    kvg_a, kvg_c = kvg_a[:rows], swap(kvg_a[rows:])
    kvg_b, kvg_d = kvg_b[:rows], swap(kvg_b[rows:])
    neigh_grad = expand(c, [kvg_a, kvg_b, kvg_c, kvg_d], weight)
    ctx = jnp.concatenate([total_of(tie(ctx_a, neigh_grad)), ctx_b], axis=1)
    mine, mate = ctx[:tokens], swap(ctx[tokens:])
    context = jnp.concatenate([jnp.where(c == 0, mine, mate), jnp.where(c == 0, mate, mine)], axis=1)
    return context, neigh_grad.reshape(block_count, block_len, feat_width)


def solution(mesh):
    parts = mesh.devices.size // (RING * RING * 2)
    fine = Mesh(mesh.devices.reshape(parts, RING, RING, 2), ("dp", "z", "y", "c"))
    every = ("dp", "z", "y", "c")
    return jax.shard_map(
        on_device,
        mesh=fine,
        in_specs=(
            P(every, None),
            P(every, None),
            P(every, None, None),
            P(every, None),
            P(("z", "y", "c"), None),
            P(every, None),
        ),
        out_specs=(P(every, None), P(every, None, None)),
        check_vma=False,
    )
```
